32 devices in a mesh: dp: 8 (over z, core), tensor: 4 (over y, x).
Axes of the slice: x: 2, y: 2, z: 4, core: 2. Of those that a mesh axis runs over, the one named last changes fastest.
Arguments:
- tokens: bfloat16 [512, 4096], P(('dp', 'tensor')), may hold values from -6 to 6
- norm_gain: float32 [4096], replicated, may hold values from 0.1 to 1.9
- gate_tiles: bfloat16 [4, 8, 256, 4096], P('tensor', 'dp'), may hold values from -0.125 to 0.125
- up_tiles: bfloat16 [4, 8, 256, 4096], P('tensor', 'dp'), may hold values from -0.125 to 0.125
- down_tiles: bfloat16 [4, 8, 256, 4096], P('tensor', 'dp'), may hold values from -0.0625 to 0.0625
- tile_ids: int32 [4, 8, 3, 256], P('tensor', 'dp'), may hold values from 0 to 447, as said below
- tile_counts: int32 [4, 8, 3], P('tensor', 'dp'), may hold values from 128 to 256, as said below
Outputs:
- mixed: bfloat16 [512, 4096], P(('dp', 'tensor'))
The draws below stay inside these ranges and needn't reach their ends.
Inputs may be any that keep to these rules, and one draw needn't show every extreme that they name: `tile_ids`: each device's slots of one matrix name distinct tiles of its shard; local tile l lies in tile row l // 56 and tile column l % 56 of the shard. `tile_counts`: only the first count slots of a matrix on a device hold kept tiles; for each matrix some device has all 256 slots kept.
All inputs are finite; a program needn't handle non-finite values.
Results may differ from the reference program's by a relative error of at most 0.014.
Values may be sent and summed in bfloat16 or wider, within the bound.
A program may use at most 256 MiB of HBM per device.

```python
import jax
import jax.numpy as jnp
from jax import lax

D = 4096
FF = 14336
TILE = 64
TOKENS = 512
ROW_TILES = 8
COL_TILES = 56
LOCAL = 448
KCAP = 256
N_DP = 8
N_TENSOR = 4


def draw_tile_ids(key, part):
    scores = jax.random.randint(key, (N_TENSOR, N_DP, 3, LOCAL), 0, 1 << 20) * LOCAL + jnp.arange(LOCAL)
    order = jnp.argsort(scores, axis=-1, stable=True)
    return order[..., :KCAP].astype(jnp.int32)


def draw_tile_counts(key, part):
    lowest = max(1, KCAP // 2)
    counts = jax.random.randint(key, (N_TENSOR * N_DP, 3), lowest, KCAP + 1)
    chosen = jax.random.randint(jax.random.fold_in(key, 7), (3,), 0, N_TENSOR * N_DP)
    hit = jnp.arange(N_TENSOR * N_DP)[:, None] == chosen[None, :]
    counts = jnp.where(hit, KCAP, counts)
    return counts.reshape(N_TENSOR, N_DP, 3).astype(jnp.int32)


def block_levels(stream_key, shape, split, least, high):
    def one(position, shards_of):
        draws = jax.random.uniform(jax.random.fold_in(jax.random.fold_in(stream_key, 6), position), (shards_of,), jnp.float32, least / len(split), high / len(split))
        return jnp.repeat(jnp.exp(draws), shape[position] // shards_of).reshape((-1,) + (1,) * (len(shape) - position - 1))

    level = one(*split[0])
    for cut in split[1:]:
        level = level * one(*cut)
    return level


def normal_values(key, dims, deviation, reach, shards=(), dtype=jnp.bfloat16):
    drawn = jax.random.normal(key, dims, jnp.float32) * deviation
    if len(shards) > 0:
        drawn = block_levels(key, dims, shards, -0.22, 0.18) * drawn
    return jnp.clip(drawn, min=-reach, max=reach).astype(dtype)


def setup_inputs(seed: int = 0) -> dict:
    keys = jax.random.split(jax.random.key(seed), 8)
    return {
        "tokens": normal_values(keys[0], (TOKENS, D), 1.0, 6.0, ((0, 32),)),
        "norm_gain": jnp.clip(1.0 + 0.18 * jax.random.normal(keys[1], (D,), jnp.float32), 0.1, 1.9),
        "gate_tiles": normal_values(keys[2], (N_TENSOR, N_DP, KCAP, TILE * TILE), (D // 2) ** -0.5, 0.125, ((0, 4), (1, 8))),
        "up_tiles": normal_values(keys[3], (N_TENSOR, N_DP, KCAP, TILE * TILE), (D // 2) ** -0.5, 0.125, ((0, 4), (1, 8))),
        "down_tiles": normal_values(keys[4], (N_TENSOR, N_DP, KCAP, TILE * TILE), (FF // 2) ** -0.5, 0.0625, ((0, 4), (1, 8))),
        "tile_ids": draw_tile_ids(jax.random.fold_in(keys[7], 71), 0),
        "tile_counts": draw_tile_counts(jax.random.fold_in(keys[7], 71), 0),
    }


def normalize(values, norm_gain):
    wide = values.astype(jnp.float32)
    meansq = lax.optimization_barrier(jnp.mean(wide * wide, axis=-1, keepdims=True))
    return (wide * lax.rsqrt(meansq + 1e-05) * norm_gain).astype(jnp.bfloat16)

def scatter_blocks(packed, slot_ids, counts, outward):
    active = (jnp.arange(KCAP)[None, :] < counts[:, None]).astype(jnp.float32)
    rows = (jnp.arange(N_DP)[:, None] * ROW_TILES + slot_ids // COL_TILES).astype(jnp.int32)
    cols = (slot_ids % COL_TILES).astype(jnp.int32)
    blocks = packed.astype(jnp.float32).reshape(N_DP, KCAP, TILE, TILE) * active[:, :, None, None]
    if outward:
        grid = jnp.zeros((COL_TILES, D // TILE, TILE, TILE), jnp.float32).at[cols, rows].add(blocks)
        return grid.transpose(0, 2, 1, 3).reshape(COL_TILES * TILE, D)
    grid = jnp.zeros((D // TILE, COL_TILES, TILE, TILE), jnp.float32).at[rows, cols].add(blocks)
    return grid.transpose(0, 2, 1, 3).reshape(D, COL_TILES * TILE)

def reference(tokens, norm_gain, gate_tiles, up_tiles, down_tiles, tile_ids, tile_counts):
    normed = normalize(tokens, norm_gain).astype(jnp.float32)

    def rank_step(summed, slices):
        gate_part, up_part, down_part, ids_part, count_part = slices
        w_gate = scatter_blocks(gate_part, ids_part[:, 0], count_part[:, 0], False)
        w_up = scatter_blocks(up_part, ids_part[:, 1], count_part[:, 1], False)
        w_down = scatter_blocks(down_part, ids_part[:, 2], count_part[:, 2], True)
        gate = jnp.dot(normed, w_gate, preferred_element_type=jnp.float32)
        upward = jnp.dot(normed, w_up, preferred_element_type=jnp.float32)
        hidden = (jax.nn.silu(gate) * upward).astype(jnp.bfloat16)
        partial_value = jnp.dot(hidden.astype(jnp.float32), w_down, preferred_element_type=jnp.float32).astype(jnp.bfloat16)
        return (summed + partial_value.astype(jnp.float32), None)
    start_sum = jnp.zeros((normed.shape[0], D), jnp.float32)
    summed, ignored = lax.scan(rank_step, start_sum, (gate_tiles, up_tiles, down_tiles, tile_ids, tile_counts))
    return summed.astype(jnp.bfloat16)
```

```python
import jax
import jax.numpy as jnp
from jax import lax
from jax.sharding import PartitionSpec as P

D = 4096
FF = 14336
TILE = 64


def normalize(values, norm_gain):
    wide = values.astype(jnp.float32)
    meansq = jnp.mean(wide * wide, axis=-1, keepdims=True)
    return (wide * lax.rsqrt(meansq + 1e-05) * norm_gain).astype(jnp.bfloat16)


def unpack_tiles(packed, slot_ids, counts, row_tiles, col_tiles):
    local_tiles = row_tiles * col_tiles
    slots = slot_ids.shape[0]
    active = jnp.arange(slots) < counts
    select = ((slot_ids[:, None] == jnp.arange(local_tiles)[None, :]) & active[:, None]).astype(
        jnp.bfloat16
    )
    placed = jnp.einsum("kl,ke->le", select, packed, preferred_element_type=jnp.float32).astype(
        jnp.bfloat16
    )
    return placed.reshape(row_tiles, col_tiles, TILE, TILE)


def inward_block(packed, slot_ids, counts, row_tiles, col_tiles):
    placed = unpack_tiles(packed, slot_ids, counts, row_tiles, col_tiles)
    return placed.transpose(0, 2, 1, 3).reshape(row_tiles * TILE, col_tiles * TILE)


def outward_block(packed, slot_ids, counts, row_tiles, col_tiles):
    placed = unpack_tiles(packed, slot_ids, counts, row_tiles, col_tiles)
    return placed.transpose(1, 2, 0, 3).reshape(col_tiles * TILE, row_tiles * TILE)


def local(tokens, norm_gain, gate_tiles, up_tiles, down_tiles, tile_ids, tile_counts):
    n_dp = lax.axis_size("dp")
    n_tensor = lax.axis_size("tensor")
    row_tiles = D // (TILE * n_dp)
    col_tiles = FF // (TILE * n_tensor)
    rows = tokens.shape[0]
    ids, counts = tile_ids[0, 0], tile_counts[0, 0]

    normed = normalize(tokens, norm_gain)
    mine = lax.all_to_all(
        normed.reshape(rows, n_dp, D // n_dp).transpose(1, 0, 2), "dp", 0, 0, tiled=True
    )
    mine = lax.all_gather(mine, "tensor", axis=1, tiled=True)
    mine = mine.reshape(n_dp * n_tensor * rows, D // n_dp)

    gate_block = inward_block(gate_tiles[0, 0], ids[0], counts[0], row_tiles, col_tiles)
    up_block = inward_block(up_tiles[0, 0], ids[1], counts[1], row_tiles, col_tiles)
    down_block = outward_block(down_tiles[0, 0], ids[2], counts[2], row_tiles, col_tiles)

    gate = jnp.dot(mine, gate_block, preferred_element_type=jnp.float32).astype(jnp.bfloat16)
    gate = lax.psum_scatter(gate, "dp", scatter_dimension=0, tiled=True)
    upward = jnp.dot(mine, up_block, preferred_element_type=jnp.float32).astype(jnp.bfloat16)
    upward = lax.psum_scatter(upward, "dp", scatter_dimension=0, tiled=True)
    hidden = (jax.nn.silu(gate.astype(jnp.float32)) * upward.astype(jnp.float32)).astype(jnp.bfloat16)
    hidden = lax.all_gather(hidden, "dp", axis=0, tiled=True)

    part = jnp.dot(hidden, down_block, preferred_element_type=jnp.float32).astype(jnp.bfloat16)
    part = lax.all_to_all(part, "dp", 0, 1, tiled=True)
    return lax.psum_scatter(part, "tensor", scatter_dimension=0, tiled=True)


def solution(mesh):
    return jax.shard_map(
        local,
        mesh=mesh,
        in_specs=(
            P(("dp", "tensor"), None),
            P(),
            P("tensor", "dp", None, None),
            P("tensor", "dp", None, None),
            P("tensor", "dp", None, None),
            P("tensor", "dp", None, None),
            P("tensor", "dp", None),
        ),
        out_specs=P(("dp", "tensor"), None),
        check_vma=False,
    )
```

```python
import jax
import jax.numpy as jnp
from jax import lax
from jax.experimental import pallas as pl
from jax.experimental.pallas import tpu as pltpu
from jax.sharding import PartitionSpec as P

D = 4096
FF = 14336
TILE = 64


def normalize(values, norm_gain):
    wide = values.astype(jnp.float32)
    meansq = jnp.mean(wide * wide, axis=-1, keepdims=True)
    return (wide * lax.rsqrt(meansq + 1e-05) * norm_gain).astype(jnp.bfloat16)


def unpack_tiles(packed, slot_ids, counts, row_tiles, col_tiles):
    local_tiles = row_tiles * col_tiles
    slots = slot_ids.shape[0]
    active = jnp.arange(slots) < counts
    select = ((slot_ids[:, None] == jnp.arange(local_tiles)[None, :]) & active[:, None]).astype(
        jnp.bfloat16
    )
    placed = jnp.einsum("kl,ke->le", select, packed, preferred_element_type=jnp.float32).astype(
        jnp.bfloat16
    )
    return placed.reshape(row_tiles, col_tiles, TILE, TILE)


def inward_block(packed, slot_ids, counts, row_tiles, col_tiles):
    placed = unpack_tiles(packed, slot_ids, counts, row_tiles, col_tiles)
    return placed.transpose(0, 2, 1, 3).reshape(row_tiles * TILE, col_tiles * TILE)


def outward_block(packed, slot_ids, counts, row_tiles, col_tiles):
    placed = unpack_tiles(packed, slot_ids, counts, row_tiles, col_tiles)
    return placed.transpose(1, 2, 0, 3).reshape(col_tiles * TILE, row_tiles * TILE)


def even_odd(width):
    source = jnp.arange(width)[:, None]
    place = jnp.arange(width)[None, :]
    inner = place % TILE
    wanted = place - inner + 2 * (inner % (TILE // 2)) + inner // (TILE // 2)
    return (source == wanted).astype(jnp.bfloat16)


def unpack_kernel(row_tiles, col_tiles, outward, ids_ref, packed_ref, out_ref, spread):
    slots = packed_ref.shape[0]
    pairs = TILE // 2
    blocks = col_tiles // 8
    tiles = row_tiles * col_tiles
    wide = 512
    tile = lax.broadcasted_iota(jnp.int32, (tiles, slots), 0)
    select = (tile == ids_ref[...]).astype(jnp.bfloat16)

    def place(step, carry):
        columns = pl.ds(pl.multiple_of(step * wide, wide), wide)
        placed = jnp.dot(select, packed_ref[:, columns], preferred_element_type=jnp.float32)
        for sub in range(wide // 128):
            for block in range(tiles // 8):
                start = block * pairs * 8 + (step * (wide // 128) + sub) * 8
                spread[pl.ds(pl.multiple_of(start, 8), 8), :] = placed[
                    block * 8 : block * 8 + 8, sub * 128 : sub * 128 + 128
                ]
        return carry

    lax.fori_loop(0, TILE * TILE // wide, place, 0)
    low = lax.broadcasted_iota(jnp.int32, (pairs, 128), 1) < TILE

    def join(left, right):
        even = jnp.where(low, left, pltpu.roll(right, TILE, 1))
        odd = jnp.where(low, pltpu.roll(left, TILE, 1), right)
        return even.astype(jnp.bfloat16), odd.astype(jnp.bfloat16)

    def build(step, carry):
        def tile_at(row, sub):
            start = (row * blocks + step // 2) * pairs * 8 + (step % 2) * 4 + sub
            return spread[pl.ds(start, pairs, stride=8), :]

        if outward:
            for sub in range(4):
                for half in range(row_tiles // 2):
                    parts = join(tile_at(2 * half, sub), tile_at(2 * half + 1, sub))
                    for odd in range(2):
                        at = sub * TILE + odd * pairs
                        out_ref[step, at : at + pairs, half * 128 : half * 128 + 128] = parts[odd]
        else:
            for row in range(row_tiles):
                for half in range(2):
                    parts = join(tile_at(row, 2 * half), tile_at(row, 2 * half + 1))
                    for odd in range(2):
                        at = row * TILE + odd * pairs
                        out_ref[step, at : at + pairs, half * 128 : half * 128 + 128] = parts[odd]
        return carry

    lax.fori_loop(0, col_tiles // 4, build, 0)


def unpack(packed, ids, row_tiles, col_tiles, outward):
    groups = col_tiles // 4
    if outward:
        shape = (groups, 4 * TILE, row_tiles * TILE)
    else:
        shape = (groups, row_tiles * TILE, 4 * TILE)
    return pl.pallas_call(
        lambda *refs: unpack_kernel(row_tiles, col_tiles, outward, *refs),
        out_shape=jax.ShapeDtypeStruct(shape, jnp.bfloat16),
        in_specs=[pl.BlockSpec(memory_space=pltpu.VMEM)] * 2,
        out_specs=pl.BlockSpec(memory_space=pltpu.VMEM),
        scratch_shapes=[pltpu.VMEM((row_tiles * col_tiles * TILE // 2, 128), jnp.float32)],
        compiler_params=pltpu.CompilerParams(vmem_limit_bytes=32 << 20),
        cost_estimate=pl.CostEstimate(flops=2 * 10**9, bytes_accessed=6 << 20, transcendentals=0),
        name="unpack_out" if outward else "unpack_in",
    )(ids, packed)


def gather_features(tokens, norm_gain):
    n_dp = lax.axis_size("dp")
    rows = tokens.shape[0]
    normed = normalize(tokens, norm_gain)
    mine = lax.all_to_all(
        normed.reshape(rows, n_dp, D // n_dp).transpose(1, 0, 2), "dp", 0, 0, tiled=True
    )
    mine = lax.all_gather(mine, "tensor", axis=1, tiled=True)
    return mine.reshape(n_dp * lax.axis_size("tensor") * rows, D // n_dp)


def spread_rows(part):
    part = lax.all_to_all(part.astype(jnp.bfloat16), "dp", 0, 1, tiled=True)
    return lax.psum_scatter(part, "tensor", scatter_dimension=0, tiled=True)


def swiglu(gate, upward):
    gate = gate.astype(jnp.float32)
    return (jax.nn.silu(gate) * upward.astype(jnp.float32)).astype(jnp.bfloat16)


def local_plain(tokens, norm_gain, gate_tiles, up_tiles, down_tiles, tile_ids, tile_counts):
    row_tiles = D // (TILE * lax.axis_size("dp"))
    col_tiles = FF // (TILE * lax.axis_size("tensor"))
    ids, counts = tile_ids[0, 0], tile_counts[0, 0]
    mine = gather_features(tokens, norm_gain)
    gate_block = inward_block(gate_tiles[0, 0], ids[0], counts[0], row_tiles, col_tiles)
    up_block = inward_block(up_tiles[0, 0], ids[1], counts[1], row_tiles, col_tiles)
    down_block = outward_block(down_tiles[0, 0], ids[2], counts[2], row_tiles, col_tiles)
    gate = jnp.dot(mine, gate_block, preferred_element_type=jnp.float32)
    gate = lax.psum_scatter(gate, "dp", scatter_dimension=0, tiled=True)
    upward = jnp.dot(mine, up_block, preferred_element_type=jnp.float32)
    upward = lax.psum_scatter(upward, "dp", scatter_dimension=0, tiled=True)
    hidden = lax.all_gather(swiglu(gate, upward), "dp", axis=0, tiled=True)
    return spread_rows(jnp.dot(hidden, down_block, preferred_element_type=jnp.float32))


def local(tokens, norm_gain, gate_tiles, up_tiles, down_tiles, tile_ids, tile_counts):
    n_dp = lax.axis_size("dp")
    row_tiles = D // (TILE * n_dp)
    col_tiles = FF // (TILE * lax.axis_size("tensor"))
    if col_tiles % 8 != 0 or row_tiles % 4 != 0:
        return local_plain(
            tokens, norm_gain, gate_tiles, up_tiles, down_tiles, tile_ids, tile_counts
        )
    slots = tile_ids.shape[-1]
    kept = jnp.arange(slots)[None, :] < tile_counts[0, 0][:, None]
    ids = jnp.where(kept, tile_ids[0, 0], -1)
    mine = gather_features(tokens, norm_gain)
    order = even_odd(256)
    mine = jnp.concatenate(
        [jnp.dot(mine[:, at : at + 256], order) for at in range(0, mine.shape[1], 256)], axis=1
    )
    gate_block = unpack(gate_tiles[0, 0], ids[0:1], row_tiles, col_tiles, False)
    up_block = unpack(up_tiles[0, 0], ids[1:2], row_tiles, col_tiles, False)
    down_block = unpack(down_tiles[0, 0], ids[2:3], row_tiles, col_tiles, True)

    def project(block):
        part = jnp.einsum("tk,gkn->gtn", mine, block, preferred_element_type=jnp.float32)
        return lax.psum_scatter(part.astype(jnp.bfloat16), "dp", scatter_dimension=1, tiled=True)

    hidden = swiglu(project(gate_block), project(up_block))
    hidden = jnp.einsum("gtn,nm->gtm", hidden, order, preferred_element_type=jnp.float32)
    hidden = lax.all_gather(hidden.astype(jnp.bfloat16), "dp", axis=1, tiled=True)
    part = jnp.einsum("gtn,gnf->tf", hidden, down_block, preferred_element_type=jnp.float32)
    return spread_rows(part)


def solution(mesh):
    return jax.shard_map(
        local,
        mesh=mesh,
        in_specs=(
            P(("dp", "tensor"), None),
            P(),
            P("tensor", "dp", None, None),
            P("tensor", "dp", None, None),
            P("tensor", "dp", None, None),
            P("tensor", "dp", None, None),
            P("tensor", "dp", None),
        ),
        out_specs=P(("dp", "tensor"), None),
        check_vma=False,
    )
```

```python
import jax
import jax.numpy as jnp
from jax import lax
from jax.experimental import pallas as pl
from jax.experimental.pallas import tpu as pltpu
from jax.sharding import PartitionSpec as P

D = 4096
FF = 14336
TILE = 64
MESH = pl.DeviceIdType.MESH


def normalize(values, norm_gain):
    wide = values.astype(jnp.float32)
    meansq = jnp.mean(wide * wide, axis=-1, keepdims=True)
    return (wide * lax.rsqrt(meansq + 1e-05) * norm_gain).astype(jnp.bfloat16)


def unpack_tiles(packed, slot_ids, counts, row_tiles, col_tiles):
    local_tiles = row_tiles * col_tiles
    slots = slot_ids.shape[0]
    active = jnp.arange(slots) < counts
    select = ((slot_ids[:, None] == jnp.arange(local_tiles)[None, :]) & active[:, None]).astype(
        jnp.bfloat16
    )
    placed = jnp.einsum("kl,ke->le", select, packed, preferred_element_type=jnp.float32).astype(
        jnp.bfloat16
    )
    return placed.reshape(row_tiles, col_tiles, TILE, TILE)


def inward_block(packed, slot_ids, counts, row_tiles, col_tiles):
    placed = unpack_tiles(packed, slot_ids, counts, row_tiles, col_tiles)
    return placed.transpose(0, 2, 1, 3).reshape(row_tiles * TILE, col_tiles * TILE)


def outward_block(packed, slot_ids, counts, row_tiles, col_tiles):
    placed = unpack_tiles(packed, slot_ids, counts, row_tiles, col_tiles)
    return placed.transpose(1, 2, 0, 3).reshape(col_tiles * TILE, row_tiles * TILE)


def even_odd(width):
    source = jnp.arange(width)[:, None]
    place = jnp.arange(width)[None, :]
    inner = place % TILE
    wanted = place - inner + 2 * (inner % (TILE // 2)) + inner // (TILE // 2)
    return (source == wanted).astype(jnp.bfloat16)


def unpack_kernel(row_tiles, col_tiles, outward, ids_ref, packed_ref, out_ref, spread):
    slots = packed_ref.shape[0]
    pairs = TILE // 2
    blocks = col_tiles // 8
    tiles = row_tiles * col_tiles
    wide = 512
    tile = lax.broadcasted_iota(jnp.int32, (tiles, slots), 0)
    select = (tile == ids_ref[...]).astype(jnp.bfloat16)

    def place(step, carry):
        columns = pl.ds(pl.multiple_of(step * wide, wide), wide)
        placed = jnp.dot(select, packed_ref[:, columns], preferred_element_type=jnp.float32)
        for sub in range(wide // 128):
            for block in range(tiles // 8):
                start = block * pairs * 8 + (step * (wide // 128) + sub) * 8
                spread[pl.ds(pl.multiple_of(start, 8), 8), :] = placed[
                    block * 8 : block * 8 + 8, sub * 128 : sub * 128 + 128
                ]
        return carry

    lax.fori_loop(0, TILE * TILE // wide, place, 0)
    low = lax.broadcasted_iota(jnp.int32, (pairs, 128), 1) < TILE

    def join(left, right):
        even = jnp.where(low, left, pltpu.roll(right, TILE, 1))
        odd = jnp.where(low, pltpu.roll(left, TILE, 1), right)
        return even.astype(jnp.bfloat16), odd.astype(jnp.bfloat16)

    def build(step, carry):
        def tile_at(row, sub):
            start = (row * blocks + step // 2) * pairs * 8 + (step % 2) * 4 + sub
            return spread[pl.ds(start, pairs, stride=8), :]

        if outward:
            for sub in range(4):
                for half in range(row_tiles // 2):
                    parts = join(tile_at(2 * half, sub), tile_at(2 * half + 1, sub))
                    for odd in range(2):
                        at = sub * TILE + odd * pairs
                        out_ref[step, at : at + pairs, half * 128 : half * 128 + 128] = parts[odd]
        else:
            for row in range(row_tiles):
                for half in range(2):
                    parts = join(tile_at(row, 2 * half), tile_at(row, 2 * half + 1))
                    for odd in range(2):
                        at = row * TILE + odd * pairs
                        out_ref[step, at : at + pairs, half * 128 : half * 128 + 128] = parts[odd]
        return carry

    lax.fori_loop(0, col_tiles // 4, build, 0)


def unpack(packed, ids, row_tiles, col_tiles, outward):
    groups = col_tiles // 4
    if outward:
        shape = (groups, 4 * TILE, row_tiles * TILE)
    else:
        shape = (groups, row_tiles * TILE, 4 * TILE)
    return pl.pallas_call(
        lambda *refs: unpack_kernel(row_tiles, col_tiles, outward, *refs),
        out_shape=jax.ShapeDtypeStruct(shape, jnp.bfloat16),
        in_specs=[pl.BlockSpec(memory_space=pltpu.VMEM)] * 2,
        out_specs=pl.BlockSpec(memory_space=pltpu.VMEM),
        scratch_shapes=[pltpu.VMEM((row_tiles * col_tiles * TILE // 2, 128), jnp.float32)],
        compiler_params=pltpu.CompilerParams(vmem_limit_bytes=32 << 20),
        cost_estimate=pl.CostEstimate(flops=2 * 10**9, bytes_accessed=6 << 20, transcendentals=0),
        name="unpack_out" if outward else "unpack_in",
    )(ids, packed)


def gather_features(tokens, norm_gain):
    n_dp = lax.axis_size("dp")
    rows = tokens.shape[0]
    normed = normalize(tokens, norm_gain)
    mine = lax.all_to_all(
        normed.reshape(rows, n_dp, D // n_dp).transpose(1, 0, 2), "dp", 0, 0, tiled=True
    )
    mine = lax.all_gather(mine, "tensor", axis=1, tiled=True)
    return mine.reshape(n_dp * lax.axis_size("tensor") * rows, D // n_dp)


def spread_rows(part):
    part = lax.all_to_all(part.astype(jnp.bfloat16), "dp", 0, 1, tiled=True)
    return lax.psum_scatter(part, "tensor", scatter_dimension=0, tiled=True)


def swiglu(gate, upward):
    gate = gate.astype(jnp.float32)
    return (jax.nn.silu(gate) * upward.astype(jnp.float32)).astype(jnp.bfloat16)


def local_plain(tokens, norm_gain, gate_tiles, up_tiles, down_tiles, tile_ids, tile_counts):
    row_tiles = D // (TILE * lax.axis_size("dp"))
    col_tiles = FF // (TILE * lax.axis_size("tensor"))
    ids, counts = tile_ids[0, 0], tile_counts[0, 0]
    mine = gather_features(tokens, norm_gain)
    gate_block = inward_block(gate_tiles[0, 0], ids[0], counts[0], row_tiles, col_tiles)
    up_block = inward_block(up_tiles[0, 0], ids[1], counts[1], row_tiles, col_tiles)
    down_block = outward_block(down_tiles[0, 0], ids[2], counts[2], row_tiles, col_tiles)
    gate = jnp.dot(mine, gate_block, preferred_element_type=jnp.float32)
    gate = lax.psum_scatter(gate, "dp", scatter_dimension=0, tiled=True)
    upward = jnp.dot(mine, up_block, preferred_element_type=jnp.float32)
    upward = lax.psum_scatter(upward, "dp", scatter_dimension=0, tiled=True)
    hidden = lax.all_gather(swiglu(gate, upward), "dp", axis=0, tiled=True)
    return spread_rows(jnp.dot(hidden, down_block, preferred_element_type=jnp.float32))


def flow_kernel(
    n_dp, n_tensor, normed, order, gate_w, up_w, down_w, out,
    xa, xg, xp, part, pair, chain, hid, acc, tail, tail_in, mixed, back,
    head_s, head_r, row_s, row_r, pair_s, pair_r, chain_s, chain_r,
    hid_s, hid_r, core_s, core_r, tail_s, tail_r, back_s, back_r,
):
    me, mt = lax.axis_index("dp"), lax.axis_index("tensor")
    z, core = me // 2, me % 2
    chips = n_dp // 2
    last = chips - 1
    groups = gate_w.shape[0]
    rows, width = xa.shape[1], xa.shape[2]
    other = 1 - core
    buddy = z * 2 + other
    hops = ((last - z, z - 1), (z, z + 1))

    barrier = pltpu.get_barrier_semaphore()
    for d in range(1, n_dp):
        pl.semaphore_signal(
            barrier, inc=1, device_id=((me + d) % n_dp, mt), device_id_type=MESH
        )
    for d in range(1, n_tensor):
        pl.semaphore_signal(
            barrier, inc=1, device_id=(me, (mt + d) % n_tensor), device_id_type=MESH
        )
    pl.semaphore_wait(barrier, n_dp + n_tensor - 2)

    def send(src, dst, send_sem, recv_sem, dp, tensor):
        return pltpu.make_async_remote_copy(
            src_ref=src, dst_ref=dst, send_sem=send_sem, recv_sem=recv_sem,
            device_id=(dp, tensor), device_id_type=MESH,
        )

    def slab(index):
        return pl.ds(pl.multiple_of(index * width, width), width)

    def head(d):
        to = (me + d) % n_dp
        return send(normed.at[:, slab(to)], xa.at[me], head_s.at[d], head_r.at[d], to, mt)

    def row(d):
        return send(xa, xg.at[mt], row_s.at[d], row_r.at[d], me, (mt + d) % n_tensor)

    for d in range(1, n_dp):
        head(d).start()
    xa[me] = normed[:, slab(me)]
    for d in range(1, n_dp):
        head(d).wait_recv()
    for d in range(1, n_tensor):
        row(d).start()
    xg[mt] = xa[...]
    for d in range(1, n_tensor):
        row(d).wait_recv()
    tokens = n_tensor * n_dp * rows
    quarter = tokens // 4
    for at in range(0, width, 256):
        xp[:, at : at + 256] = jnp.dot(
            xg[:, :, :, at : at + 256].reshape(tokens, 256),
            order[...],
            preferred_element_type=jnp.float32,
        ).astype(jnp.bfloat16)
    acc[...] = jnp.zeros_like(acc)

    def pair_copy(n):
        return send(part.at[n, :, other], pair.at[n], pair_s.at[n], pair_r.at[n], buddy, mt)

    def chain_copy(n, h):
        return send(
            part.at[n, h, core], chain.at[n, h], chain_s.at[n, h], chain_r.at[n, h],
            jnp.clip(hops[h][1], 0, last) * 2 + core, mt,
        )

    def hid_copy(n, h):
        to = jnp.clip(hops[1 - h][1], 0, last) * 2 + core
        return send(
            hid.at[n, h, core], hid.at[n, h, core], hid_s.at[n, h], hid_r.at[n, h], to, mt
        )

    def core_copy(n, h):
        return send(
            hid.at[n, h, core], hid.at[n, h, core], core_s.at[n, h], core_r.at[n, h], buddy, mt
        )

    def project(n):
        for which, weight in enumerate((gate_w, up_w)):
            value = jnp.dot(xp[...], weight[n], preferred_element_type=jnp.float32)
            part[n, :, :, :, which * 256 : which * 256 + 256] = value.astype(
                jnp.bfloat16
            ).reshape(2, 2, quarter, 256)
        pair_copy(n).start()

    def inside(n):
        return (n >= 0) & (n < groups)

    ahead = 2
    for n in range(ahead):
        project(jnp.int32(n))
    nearest = jnp.minimum(z, last - z)
    farthest = jnp.maximum(z, last - z)

    def step(s, carry):
        @pl.when(inside(s - nearest))
        def _():
            pair_copy(s - nearest).wait_recv()

        for h in range(2):
            position = hops[h][0]
            n = s - position

            @pl.when(inside(n))
            def _():
                def own():
                    return part[n, h, core].astype(jnp.float32) + pair[n, h].astype(jnp.float32)

                @pl.when(position > 0)
                def _():
                    chain_copy(n, h).wait_recv()

                @pl.when(position == 0)
                def _():
                    part[n, h, core] = own().astype(jnp.bfloat16)

                @pl.when((position > 0) & (position < last))
                def _():
                    part[n, h, core] = (own() + chain[n, h].astype(jnp.float32)).astype(jnp.bfloat16)

                @pl.when(position < last)
                def _():
                    chain_copy(n, h).start()

                @pl.when(position == last)
                def _():
                    total = own() + chain[n, h].astype(jnp.float32)
                    gate = total[:, :256]
                    value = gate / (1.0 + jnp.exp(-gate)) * total[:, 256:]
                    hid[n, h, core] = jnp.dot(
                        value.astype(jnp.bfloat16), order[...], preferred_element_type=jnp.float32
                    ).astype(jnp.bfloat16)

        for h in range(2):
            distance = last - hops[h][0]
            n = s - last - distance

            @pl.when(inside(n))
            def _():
                @pl.when(distance > 0)
                def _():
                    hid_copy(n, h).wait_recv()

                @pl.when(distance < last)
                def _():
                    hid_copy(n, h).start()

                core_copy(n, h).start()

        @pl.when(s + ahead < groups)
        def _():
            project(s + ahead)

        done = s - last - farthest - 1

        @pl.when(inside(done))
        def _():
            for h in range(2):
                core_copy(done, h).wait_recv()
            acc[...] += jnp.dot(
                hid[done].reshape(tokens, 256), down_w[done], preferred_element_type=jnp.float32
            )

        return carry

    lax.fori_loop(0, groups + 2 * last + 1, step, 0)

    tail[...] = acc[...].astype(jnp.bfloat16).reshape(tail.shape)

    def tail_copy(d):
        to = (mt + d) % n_tensor
        return send(tail.at[to], tail_in.at[mt], tail_s.at[d], tail_r.at[d], me, to)

    def back_copy(d):
        to = (me + d) % n_dp
        return send(mixed.at[to], back.at[me], back_s.at[d], back_r.at[d], to, mt)

    for d in range(1, n_tensor):
        tail_copy(d).start()
    tail_in[mt] = tail[mt]
    for d in range(1, n_tensor):
        tail_copy(d).wait_recv()
    total = tail_in[0].astype(jnp.float32)
    for t in range(1, n_tensor):
        total += tail_in[t].astype(jnp.float32)
    mixed[...] = total.astype(jnp.bfloat16).reshape(mixed.shape)
    for d in range(1, n_dp):
        back_copy(d).start()
    back[me] = mixed[me]

    def drain(n, carry):
        pair_copy(n).wait_send()
        for h in range(2):
            core_copy(n, h).wait_send()

            @pl.when(hops[h][0] < last)
            def _():
                chain_copy(n, h).wait_send()

            @pl.when(last - hops[h][0] < last)
            def _():
                hid_copy(n, h).wait_send()

        return carry

    lax.fori_loop(0, groups, drain, 0)
    for d in range(1, n_dp):
        head(d).wait_send()
        back_copy(d).wait_recv()
        back_copy(d).wait_send()
    for d in range(1, n_tensor):
        row(d).wait_send()
        tail_copy(d).wait_send()
    for p in range(n_dp):
        out[:, p * width : p * width + width] = back[p]


def flow(normed, order, gate_w, up_w, down_w, n_dp, n_tensor):
    groups, width, _ = gate_w.shape
    rows = normed.shape[0]
    tokens = rows * n_dp * n_tensor
    quarter = tokens // 4
    half = jnp.bfloat16
    dma = pltpu.SemaphoreType.DMA
    return pl.pallas_call(
        lambda *refs: flow_kernel(n_dp, n_tensor, *refs),
        out_shape=jax.ShapeDtypeStruct(normed.shape, half),
        in_specs=[pl.BlockSpec(memory_space=pltpu.VMEM)] * 5,
        out_specs=pl.BlockSpec(memory_space=pltpu.VMEM),
        scratch_shapes=[
            pltpu.VMEM((n_dp, rows, width), half),
            pltpu.VMEM((n_tensor, n_dp, rows, width), half),
            pltpu.VMEM((tokens, width), half),
            pltpu.VMEM((groups, 2, 2, quarter, 512), half),
            pltpu.VMEM((groups, 2, quarter, 512), half),
            pltpu.VMEM((groups, 2, quarter, 512), half),
            pltpu.VMEM((groups, 2, 2, quarter, 256), half),
            pltpu.VMEM((tokens, width), jnp.float32),
            pltpu.VMEM((n_tensor, n_dp * rows, width), half),
            pltpu.VMEM((n_tensor, n_dp * rows, width), half),
            pltpu.VMEM((n_dp, rows, width), half),
            pltpu.VMEM((n_dp, rows, width), half),
            dma((n_dp,)), dma((n_dp,)), dma((n_tensor,)), dma((n_tensor,)),
            dma((groups,)), dma((groups,)), dma((groups, 2)), dma((groups, 2)),
            dma((groups, 2)), dma((groups, 2)), dma((groups, 2)), dma((groups, 2)),
            dma((n_tensor,)), dma((n_tensor,)), dma((n_dp,)), dma((n_dp,)),
        ],
        compiler_params=pltpu.CompilerParams(
            collective_id=0, has_side_effects=True, vmem_limit_bytes=56 << 20
        ),
        cost_estimate=pl.CostEstimate(
            flops=6 * 10**9, bytes_accessed=12 << 20, transcendentals=10**6
        ),
        name="flow",
    )(normed, order, gate_w, up_w, down_w)


def local(tokens, norm_gain, gate_tiles, up_tiles, down_tiles, tile_ids, tile_counts):
    n_dp, n_tensor = lax.axis_size("dp"), lax.axis_size("tensor")
    row_tiles = D // (TILE * n_dp)
    col_tiles = FF // (TILE * n_tensor)
    if col_tiles % 8 != 0 or row_tiles % 4 != 0 or n_tensor != 4 or n_dp % 2 != 0:
        return local_plain(
            tokens, norm_gain, gate_tiles, up_tiles, down_tiles, tile_ids, tile_counts
        )
    slots = tile_ids.shape[-1]
    kept = jnp.arange(slots)[None, :] < tile_counts[0, 0][:, None]
    ids = jnp.where(kept, tile_ids[0, 0], -1)
    gate_w = unpack(gate_tiles[0, 0], ids[0:1], row_tiles, col_tiles, False)
    up_w = unpack(up_tiles[0, 0], ids[1:2], row_tiles, col_tiles, False)
    down_w = unpack(down_tiles[0, 0], ids[2:3], row_tiles, col_tiles, True)
    normed = normalize(tokens, norm_gain)
    return flow(normed, even_odd(256), gate_w, up_w, down_w, n_dp, n_tensor)


def solution(mesh):
    return jax.shard_map(
        local,
        mesh=mesh,
        in_specs=(
            P(("dp", "tensor"), None),
            P(),
            P("tensor", "dp", None, None),
            P("tensor", "dp", None, None),
            P("tensor", "dp", None, None),
            P("tensor", "dp", None, None),
            P("tensor", "dp", None),
        ),
        out_specs=P(("dp", "tensor"), None),
        check_vma=False,
    )
```

```python
import jax
import jax.numpy as jnp
from jax import lax
from jax.experimental import pallas as pl
from jax.experimental.pallas import tpu as pltpu
from jax.sharding import PartitionSpec as P

D = 4096
FF = 14336
TILE = 64
MESH = pl.DeviceIdType.MESH


def normalize(values, norm_gain):
    wide = values.astype(jnp.float32)
    meansq = jnp.mean(wide * wide, axis=-1, keepdims=True)
    return (wide * lax.rsqrt(meansq + 1e-05) * norm_gain).astype(jnp.bfloat16)


def unpack_tiles(packed, slot_ids, counts, row_tiles, col_tiles):
    local_tiles = row_tiles * col_tiles
    slots = slot_ids.shape[0]
    active = jnp.arange(slots) < counts
    select = ((slot_ids[:, None] == jnp.arange(local_tiles)[None, :]) & active[:, None]).astype(
        jnp.bfloat16
    )
    placed = jnp.einsum("kl,ke->le", select, packed, preferred_element_type=jnp.float32).astype(
        jnp.bfloat16
    )
    return placed.reshape(row_tiles, col_tiles, TILE, TILE)


def inward_block(packed, slot_ids, counts, row_tiles, col_tiles):
    placed = unpack_tiles(packed, slot_ids, counts, row_tiles, col_tiles)
    return placed.transpose(0, 2, 1, 3).reshape(row_tiles * TILE, col_tiles * TILE)


def outward_block(packed, slot_ids, counts, row_tiles, col_tiles):
    placed = unpack_tiles(packed, slot_ids, counts, row_tiles, col_tiles)
    return placed.transpose(1, 2, 0, 3).reshape(col_tiles * TILE, row_tiles * TILE)


def gather_features(tokens, norm_gain):
    n_dp = lax.axis_size("dp")
    rows = tokens.shape[0]
    normed = normalize(tokens, norm_gain)
    mine = lax.all_to_all(
        normed.reshape(rows, n_dp, D // n_dp).transpose(1, 0, 2), "dp", 0, 0, tiled=True
    )
    mine = lax.all_gather(mine, "tensor", axis=1, tiled=True)
    return mine.reshape(n_dp * lax.axis_size("tensor") * rows, D // n_dp)


def spread_rows(part):
    part = lax.all_to_all(part.astype(jnp.bfloat16), "dp", 0, 1, tiled=True)
    return lax.psum_scatter(part, "tensor", scatter_dimension=0, tiled=True)


def swiglu(gate, upward):
    gate = gate.astype(jnp.float32)
    return (jax.nn.silu(gate) * upward.astype(jnp.float32)).astype(jnp.bfloat16)


def local_plain(tokens, norm_gain, gate_tiles, up_tiles, down_tiles, tile_ids, tile_counts):
    row_tiles = D // (TILE * lax.axis_size("dp"))
    col_tiles = FF // (TILE * lax.axis_size("tensor"))
    ids, counts = tile_ids[0, 0], tile_counts[0, 0]
    mine = gather_features(tokens, norm_gain)
    gate_block = inward_block(gate_tiles[0, 0], ids[0], counts[0], row_tiles, col_tiles)
    up_block = inward_block(up_tiles[0, 0], ids[1], counts[1], row_tiles, col_tiles)
    down_block = outward_block(down_tiles[0, 0], ids[2], counts[2], row_tiles, col_tiles)
    gate = jnp.dot(mine, gate_block, preferred_element_type=jnp.float32)
    gate = lax.psum_scatter(gate, "dp", scatter_dimension=0, tiled=True)
    upward = jnp.dot(mine, up_block, preferred_element_type=jnp.float32)
    upward = lax.psum_scatter(upward, "dp", scatter_dimension=0, tiled=True)
    hidden = lax.all_gather(swiglu(gate, upward), "dp", axis=0, tiled=True)
    return spread_rows(jnp.dot(hidden, down_block, preferred_element_type=jnp.float32))


LAG = 2
WIDE = 512


def flow_kernel(
    n_dp, n_tensor, row_tiles, col_tiles,
    tokens_in, gain, ids, counts, gate_p, up_p, down_p, out,
    normed, order, packed, gate_t, up_t, down_t, inward_w, down_w,
    xa, xg, xp, part, pair, chain, hid, acc, tail, tail_in, mixed, back, load_s,
    head_s, head_r, row_s, row_r, pair_s, pair_r, chain_s, chain_r,
    hid_s, hid_r, core_s, core_r, tail_s, tail_r, back_s, back_r,
):
    me, mt = lax.axis_index("dp"), lax.axis_index("tensor")
    z, core = me // 2, me % 2
    chips = n_dp // 2
    last = chips - 1
    groups = part.shape[0]
    rows, width = xa.shape[1], xa.shape[2]
    other = 1 - core
    buddy = z * 2 + other
    hops = ((last - z, z - 1), (z, z + 1))

    barrier = pltpu.get_barrier_semaphore()
    for d in range(1, n_dp):
        pl.semaphore_signal(
            barrier, inc=1, device_id=((me + d) % n_dp, mt), device_id_type=MESH
        )
    for d in range(1, n_tensor):
        pl.semaphore_signal(
            barrier, inc=1, device_id=(me, (mt + d) % n_tensor), device_id_type=MESH
        )
    loads = [
        pltpu.make_async_copy(source, packed.at[i], load_s.at[i])
        for i, source in enumerate((gate_p, up_p, down_p))
    ]
    for load in loads:
        load.start()

    wide = tokens_in[...].astype(jnp.float32)
    meansq = jnp.mean(wide * wide, axis=-1, keepdims=True)
    normed[...] = (wide * lax.rsqrt(meansq + 1e-05) * gain[...]).astype(jnp.bfloat16)
    source = lax.broadcasted_iota(jnp.int32, (256, 256), 0)
    place = lax.broadcasted_iota(jnp.int32, (256, 256), 1)
    inner = place & (TILE - 1)
    wanted = place - inner + 2 * (inner & (TILE // 2 - 1)) + (inner >> 5)
    order[...] = (source == wanted).astype(jnp.bfloat16)
    pl.semaphore_wait(barrier, n_dp + n_tensor - 2)

    pairs = TILE // 2
    blocks = col_tiles // 8
    tiles = row_tiles * col_tiles
    slots = packed.shape[1]
    low = lax.broadcasted_iota(jnp.int32, (pairs, 128), 1) < TILE

    def place_tiles(which, spread, at):
        tile = lax.broadcasted_iota(jnp.int32, (tiles, slots), 0)
        slot = lax.broadcasted_iota(jnp.int32, (tiles, slots), 1)
        hit = (tile == ids[which : which + 1, :]) & (slot < counts[which : which + 1, :])
        columns = pl.ds(pl.multiple_of(at * WIDE, WIDE), WIDE)
        placed = jnp.dot(
            hit.astype(jnp.bfloat16), packed[which, :, columns], preferred_element_type=jnp.float32
        )
        for sub in range(WIDE // 128):
            for block in range(tiles // 8):
                start = block * pairs * 8 + (at * (WIDE // 128) + sub) * 8
                spread[pl.ds(pl.multiple_of(start, 8), 8), :] = placed[
                    block * 8 : block * 8 + 8, sub * 128 : sub * 128 + 128
                ]

    def place_all(which, spread):
        def body(at, carry):
            place_tiles(which, spread, at)
            return carry

        lax.fori_loop(0, TILE * TILE // WIDE, body, 0)

    def tile_at(spread, n, row, sub):
        start = (row * blocks + n // 4) * pairs * 8 + (n % 4) * 2 + sub
        return spread[pl.ds(start, pairs, stride=8), :]

    def join(left, right):
        even = jnp.where(low, left, pltpu.roll(right, TILE, 1))
        odd = jnp.where(low, pltpu.roll(left, TILE, 1), right)
        return even.astype(jnp.bfloat16), odd.astype(jnp.bfloat16)

    def build_inward(n):
        for which, spread in enumerate((gate_t, up_t)):
            for row in range(row_tiles):
                both = join(tile_at(spread, n, row, 0), tile_at(spread, n, row, 1))
                for odd in range(2):
                    at = row * TILE + odd * pairs
                    inward_w[at : at + pairs, which * 128 : which * 128 + 128] = both[odd]

    def build_down(n):
        for sub in range(2):
            for half in range(row_tiles // 2):
                both = join(
                    tile_at(down_t, n, 2 * half, sub), tile_at(down_t, n, 2 * half + 1, sub)
                )
                for odd in range(2):
                    at = sub * TILE + odd * pairs
                    down_w[at : at + pairs, half * 128 : half * 128 + 128] = both[odd]

    def send(src, dst, send_sem, recv_sem, dp, tensor):
        return pltpu.make_async_remote_copy(
            src_ref=src, dst_ref=dst, send_sem=send_sem, recv_sem=recv_sem,
            device_id=(dp, tensor), device_id_type=MESH,
        )

    def slab(index):
        return pl.ds(pl.multiple_of(index * width, width), width)

    def head(d):
        to = (me + d) % n_dp
        return send(normed.at[:, slab(to)], xa.at[me], head_s.at[d], head_r.at[d], to, mt)

    def row(d):
        return send(xa, xg.at[mt], row_s.at[d], row_r.at[d], me, (mt + d) % n_tensor)

    for d in range(1, n_dp):
        head(d).start()
    xa[me] = normed[:, slab(me)]
    loads[0].wait()
    place_all(0, gate_t)
    for d in range(1, n_dp):
        head(d).wait_recv()
    for d in range(1, n_tensor):
        row(d).start()
    xg[mt] = xa[...]
    loads[1].wait()
    place_all(1, up_t)
    for d in range(1, n_tensor):
        row(d).wait_recv()
    tokens = n_tensor * n_dp * rows
    quarter = tokens // 4
    for at in range(0, width, 256):
        xp[:, at : at + 256] = jnp.dot(
            xg[:, :, :, at : at + 256].reshape(tokens, 256),
            order[...],
            preferred_element_type=jnp.float32,
        ).astype(jnp.bfloat16)
    acc[...] = jnp.zeros_like(acc)
    loads[2].wait()

    def pair_copy(n):
        return send(part.at[n, :, other], pair.at[n], pair_s.at[n], pair_r.at[n], buddy, mt)

    def chain_copy(n, h):
        return send(
            part.at[n, h, core], chain.at[n, h], chain_s.at[n, h], chain_r.at[n, h],
            jnp.clip(hops[h][1], 0, last) * 2 + core, mt,
        )

    def hid_copy(n, h):
        to = jnp.clip(hops[1 - h][1], 0, last) * 2 + core
        return send(
            hid.at[n, h, core], hid.at[n, h, core], hid_s.at[n, h], hid_r.at[n, h], to, mt
        )

    def core_copy(n, h):
        return send(
            hid.at[n, h, core], hid.at[n, h, core], core_s.at[n, h], core_r.at[n, h], buddy, mt
        )

    def project(n):
        build_inward(n)
        value = jnp.dot(xp[...], inward_w[...], preferred_element_type=jnp.float32)
        part[n] = value.astype(jnp.bfloat16).reshape(2, 2, quarter, 256)
        pair_copy(n).start()

    def inside(n):
        return (n >= 0) & (n < groups)

    ahead = 2
    for n in range(ahead):
        project(jnp.int32(n))
    nearest = jnp.minimum(z, last - z)
    farthest = jnp.maximum(z, last - z)

    def step(s, carry):
        @pl.when(inside(s - LAG * nearest))
        def _():
            pair_copy(s - LAG * nearest).wait_recv()

        for h in range(2):
            position = hops[h][0]
            n = s - LAG * position

            @pl.when(inside(n))
            def _():
                def own():
                    return part[n, h, core].astype(jnp.float32) + pair[n, h].astype(jnp.float32)

                @pl.when(position > 0)
                def _():
                    chain_copy(n, h).wait_recv()

                @pl.when(position == 0)
                def _():
                    part[n, h, core] = own().astype(jnp.bfloat16)

                @pl.when((position > 0) & (position < last))
                def _():
                    part[n, h, core] = (own() + chain[n, h].astype(jnp.float32)).astype(jnp.bfloat16)

                @pl.when(position < last)
                def _():
                    chain_copy(n, h).start()

                @pl.when(position == last)
                def _():
                    total = own() + chain[n, h].astype(jnp.float32)
                    gate = total[:, :128]
                    value = gate / (1.0 + jnp.exp(-gate)) * total[:, 128:]
                    hid[n, h, core] = jnp.dot(
                        value.astype(jnp.bfloat16), order[:128, :128], preferred_element_type=jnp.float32
                    ).astype(jnp.bfloat16)

        for h in range(2):
            distance = last - hops[h][0]
            n = s - LAG * (last + distance)

            @pl.when(inside(n))
            def _():
                @pl.when(distance > 0)
                def _():
                    hid_copy(n, h).wait_recv()

                @pl.when(distance < last)
                def _():
                    hid_copy(n, h).start()

                core_copy(n, h).start()

        @pl.when(s + ahead < groups)
        def _():
            project(s + ahead)

        @pl.when(s < TILE * TILE // WIDE)
        def _():
            place_tiles(2, down_t, s)

        done = s - LAG * (last + farthest) - 1

        @pl.when(inside(done))
        def _():
            for h in range(2):
                core_copy(done, h).wait_recv()
            build_down(done)
            acc[...] += jnp.dot(
                hid[done].reshape(tokens, 128), down_w[...], preferred_element_type=jnp.float32
            )

        return carry

    lax.fori_loop(0, groups + 2 * LAG * last + 1, step, 0)

    tail[...] = acc[...].astype(jnp.bfloat16).reshape(tail.shape)

    def tail_copy(d):
        to = (mt + d) % n_tensor
        return send(tail.at[to], tail_in.at[mt], tail_s.at[d], tail_r.at[d], me, to)

    def back_copy(d):
        to = (me + d) % n_dp
        return send(mixed.at[to], back.at[me], back_s.at[d], back_r.at[d], to, mt)

    for d in range(1, n_tensor):
        tail_copy(d).start()
    tail_in[mt] = tail[mt]
    for d in range(1, n_tensor):
        tail_copy(d).wait_recv()
    total = tail_in[0].astype(jnp.float32)
    for t in range(1, n_tensor):
        total += tail_in[t].astype(jnp.float32)
    mixed[...] = total.astype(jnp.bfloat16).reshape(mixed.shape)
    for d in range(1, n_dp):
        back_copy(d).start()
    back[me] = mixed[me]

    def drain(n, carry):
        pair_copy(n).wait_send()
        for h in range(2):
            core_copy(n, h).wait_send()

            @pl.when(hops[h][0] < last)
            def _():
                chain_copy(n, h).wait_send()

            @pl.when(last - hops[h][0] < last)
            def _():
                hid_copy(n, h).wait_send()

        return carry

    lax.fori_loop(0, groups, drain, 0)
    for d in range(1, n_dp):
        head(d).wait_send()
        back_copy(d).wait_recv()
        back_copy(d).wait_send()
    for d in range(1, n_tensor):
        row(d).wait_send()
        tail_copy(d).wait_send()
    for p in range(n_dp):
        out[:, p * width : p * width + width] = back[p]


def flow(tokens, gain, ids, counts, gate_p, up_p, down_p, n_dp, n_tensor, row_tiles, col_tiles):
    groups = col_tiles // 2
    width = row_tiles * TILE
    rows = tokens.shape[0]
    total = rows * n_dp * n_tensor
    quarter = total // 4
    tiles = row_tiles * col_tiles
    half = jnp.bfloat16
    dma = pltpu.SemaphoreType.DMA
    vmem = pl.BlockSpec(memory_space=pltpu.VMEM)
    return pl.pallas_call(
        lambda *refs: flow_kernel(n_dp, n_tensor, row_tiles, col_tiles, *refs),
        out_shape=jax.ShapeDtypeStruct(tokens.shape, half),
        in_specs=[vmem] * 4 + [pl.BlockSpec(memory_space=pl.ANY)] * 3,
        out_specs=vmem,
        scratch_shapes=[
            pltpu.VMEM(tokens.shape, half),
            pltpu.VMEM((256, 256), half),
            pltpu.VMEM((3,) + gate_p.shape, half),
            pltpu.VMEM((tiles * TILE // 2, 128), jnp.float32),
            pltpu.VMEM((tiles * TILE // 2, 128), jnp.float32),
            pltpu.VMEM((tiles * TILE // 2, 128), jnp.float32),
            pltpu.VMEM((width, 256), half),
            pltpu.VMEM((128, width), half),
            pltpu.VMEM((n_dp, rows, width), half),
            pltpu.VMEM((n_tensor, n_dp, rows, width), half),
            pltpu.VMEM((total, width), half),
            pltpu.VMEM((groups, 2, 2, quarter, 256), half),
            pltpu.VMEM((groups, 2, quarter, 256), half),
            pltpu.VMEM((groups, 2, quarter, 256), half),
            pltpu.VMEM((groups, 2, 2, quarter, 128), half),
            pltpu.VMEM((total, width), jnp.float32),
            pltpu.VMEM((n_tensor, n_dp * rows, width), half),
            pltpu.VMEM((n_tensor, n_dp * rows, width), half),
            pltpu.VMEM((n_dp, rows, width), half),
            pltpu.VMEM((n_dp, rows, width), half),
            dma((3,)),
            dma((n_dp,)), dma((n_dp,)), dma((n_tensor,)), dma((n_tensor,)),
            dma((groups,)), dma((groups,)), dma((groups, 2)), dma((groups, 2)),
            dma((groups, 2)), dma((groups, 2)), dma((groups, 2)), dma((groups, 2)),
            dma((n_tensor,)), dma((n_tensor,)), dma((n_dp,)), dma((n_dp,)),
        ],
        compiler_params=pltpu.CompilerParams(
            collective_id=0, has_side_effects=True, vmem_limit_bytes=60 << 20
        ),
        cost_estimate=pl.CostEstimate(
            flops=9 * 10**9, bytes_accessed=6 << 20, transcendentals=10**6
        ),
        name="flow",
    )(tokens, gain, ids, counts, gate_p, up_p, down_p)


def local(tokens, norm_gain, gate_tiles, up_tiles, down_tiles, tile_ids, tile_counts):
    n_dp, n_tensor = lax.axis_size("dp"), lax.axis_size("tensor")
    row_tiles = D // (TILE * n_dp)
    col_tiles = FF // (TILE * n_tensor)
    if col_tiles % 8 != 0 or row_tiles % 4 != 0 or n_tensor != 4 or n_dp != 8:
        return local_plain(
            tokens, norm_gain, gate_tiles, up_tiles, down_tiles, tile_ids, tile_counts
        )
    return flow(
        tokens, norm_gain[None, :], tile_ids[0, 0], tile_counts[0, 0][:, None],
        gate_tiles[0, 0], up_tiles[0, 0], down_tiles[0, 0],
        n_dp, n_tensor, row_tiles, col_tiles,
    )


def solution(mesh):
    return jax.shard_map(
        local,
        mesh=mesh,
        in_specs=(
            P(("dp", "tensor"), None),
            P(),
            P("tensor", "dp", None, None),
            P("tensor", "dp", None, None),
            P("tensor", "dp", None, None),
            P("tensor", "dp", None, None),
            P("tensor", "dp", None),
        ),
        out_specs=P(("dp", "tensor"), None),
        check_vma=False,
    )
```

```python
import jax
import jax.numpy as jnp
from jax import lax
from jax.experimental import pallas as pl
from jax.experimental.pallas import tpu as pltpu
from jax.sharding import PartitionSpec as P

D = 4096
FF = 14336
TILE = 64
MESH = pl.DeviceIdType.MESH


def normalize(values, norm_gain):
    wide = values.astype(jnp.float32)
    meansq = jnp.mean(wide * wide, axis=-1, keepdims=True)
    return (wide * lax.rsqrt(meansq + 1e-05) * norm_gain).astype(jnp.bfloat16)


def unpack_tiles(packed, slot_ids, counts, row_tiles, col_tiles):
    local_tiles = row_tiles * col_tiles
    slots = slot_ids.shape[0]
    active = jnp.arange(slots) < counts
    select = ((slot_ids[:, None] == jnp.arange(local_tiles)[None, :]) & active[:, None]).astype(
        jnp.bfloat16
    )
    placed = jnp.einsum("kl,ke->le", select, packed, preferred_element_type=jnp.float32).astype(
        jnp.bfloat16
    )
    return placed.reshape(row_tiles, col_tiles, TILE, TILE)


def inward_block(packed, slot_ids, counts, row_tiles, col_tiles):
    placed = unpack_tiles(packed, slot_ids, counts, row_tiles, col_tiles)
    return placed.transpose(0, 2, 1, 3).reshape(row_tiles * TILE, col_tiles * TILE)


def outward_block(packed, slot_ids, counts, row_tiles, col_tiles):
    placed = unpack_tiles(packed, slot_ids, counts, row_tiles, col_tiles)
    return placed.transpose(1, 2, 0, 3).reshape(col_tiles * TILE, row_tiles * TILE)


def gather_features(tokens, norm_gain):
    n_dp = lax.axis_size("dp")
    rows = tokens.shape[0]
    normed = normalize(tokens, norm_gain)
    mine = lax.all_to_all(
        normed.reshape(rows, n_dp, D // n_dp).transpose(1, 0, 2), "dp", 0, 0, tiled=True
    )
    mine = lax.all_gather(mine, "tensor", axis=1, tiled=True)
    return mine.reshape(n_dp * lax.axis_size("tensor") * rows, D // n_dp)


def spread_rows(part):
    part = lax.all_to_all(part.astype(jnp.bfloat16), "dp", 0, 1, tiled=True)
    return lax.psum_scatter(part, "tensor", scatter_dimension=0, tiled=True)


def swiglu(gate, upward):
    gate = gate.astype(jnp.float32)
    return (jax.nn.silu(gate) * upward.astype(jnp.float32)).astype(jnp.bfloat16)


def local_plain(tokens, norm_gain, gate_tiles, up_tiles, down_tiles, tile_ids, tile_counts):
    row_tiles = D // (TILE * lax.axis_size("dp"))
    col_tiles = FF // (TILE * lax.axis_size("tensor"))
    ids, counts = tile_ids[0, 0], tile_counts[0, 0]
    mine = gather_features(tokens, norm_gain)
    gate_block = inward_block(gate_tiles[0, 0], ids[0], counts[0], row_tiles, col_tiles)
    up_block = inward_block(up_tiles[0, 0], ids[1], counts[1], row_tiles, col_tiles)
    down_block = outward_block(down_tiles[0, 0], ids[2], counts[2], row_tiles, col_tiles)
    gate = jnp.dot(mine, gate_block, preferred_element_type=jnp.float32)
    gate = lax.psum_scatter(gate, "dp", scatter_dimension=0, tiled=True)
    upward = jnp.dot(mine, up_block, preferred_element_type=jnp.float32)
    upward = lax.psum_scatter(upward, "dp", scatter_dimension=0, tiled=True)
    hidden = lax.all_gather(swiglu(gate, upward), "dp", axis=0, tiled=True)
    return spread_rows(jnp.dot(hidden, down_block, preferred_element_type=jnp.float32))


LAG = 2
WIDE = 512


def flow_kernel(
    n_dp, n_tensor, row_tiles, col_tiles,
    tokens_in, gain, ids, counts, gate_p, up_p, down_p, out,
    normed, order, packed, gate_t, up_t, down_t, inward_w, down_w,
    xa, xg, xp, part, pair, chain, hid, acc, tail, tail_in, mixed, back, load_s,
    head_s, head_r, row_s, row_r, pair_s, pair_r, chain_s, chain_r,
    hid_s, hid_r, core_s, core_r, tail_s, tail_r, back_s, back_r,
):
    me, mt = lax.axis_index("dp"), lax.axis_index("tensor")
    z, core = me // 2, me % 2
    chips = n_dp // 2
    last = chips - 1
    groups = part.shape[0]
    rows, width = xa.shape[1], xa.shape[2]
    other = 1 - core
    buddy = z * 2 + other
    hops = ((last - z, z - 1), (z, z + 1))

    barrier = pltpu.get_barrier_semaphore()
    for d in range(1, n_dp):
        pl.semaphore_signal(
            barrier, inc=1, device_id=((me + d) % n_dp, mt), device_id_type=MESH
        )
    for d in range(1, n_tensor):
        pl.semaphore_signal(
            barrier, inc=1, device_id=(me, (mt + d) % n_tensor), device_id_type=MESH
        )
    loads = [
        pltpu.make_async_copy(source, packed.at[i], load_s.at[i])
        for i, source in enumerate((gate_p, up_p, down_p))
    ]
    for load in loads:
        load.start()

    wide = tokens_in[...].astype(jnp.float32)
    meansq = jnp.mean(wide * wide, axis=-1, keepdims=True)
    normed[...] = (wide * lax.rsqrt(meansq + 1e-05) * gain[...].reshape(1, D)).astype(jnp.bfloat16)
    source = lax.broadcasted_iota(jnp.int32, (256, 256), 0)
    place = lax.broadcasted_iota(jnp.int32, (256, 256), 1)
    inner = place & (TILE - 1)
    wanted = place - inner + 2 * (inner & (TILE // 2 - 1)) + (inner >> 5)
    order[...] = (source == wanted).astype(jnp.bfloat16)
    pl.semaphore_wait(barrier, n_dp + n_tensor - 2)

    pairs = TILE // 2
    blocks = col_tiles // 8
    tiles = row_tiles * col_tiles
    slots = packed.shape[1]
    low = lax.broadcasted_iota(jnp.int32, (pairs, 128), 1) < TILE

    def place_tiles(which, spread, at):
        tile = lax.broadcasted_iota(jnp.int32, (tiles, slots), 0)
        slot = lax.broadcasted_iota(jnp.int32, (tiles, slots), 1)
        hit = (tile == ids[which]) & (slot < counts[0, 0, which])
        columns = pl.ds(pl.multiple_of(at * WIDE, WIDE), WIDE)
        placed = jnp.dot(
            hit.astype(jnp.bfloat16), packed[which, :, columns], preferred_element_type=jnp.float32
        )
        for sub in range(WIDE // 128):
            for block in range(tiles // 8):
                start = block * pairs * 8 + (at * (WIDE // 128) + sub) * 8
                spread[pl.ds(pl.multiple_of(start, 8), 8), :] = placed[
                    block * 8 : block * 8 + 8, sub * 128 : sub * 128 + 128
                ]

    def place_all(which, spread):
        def body(at, carry):
            place_tiles(which, spread, at)
            return carry

        lax.fori_loop(0, TILE * TILE // WIDE, body, 0)

    def tile_at(spread, n, row, sub):
        start = (row * blocks + n // 4) * pairs * 8 + (n % 4) * 2 + sub
        return spread[pl.ds(start, pairs, stride=8), :]

    def join(left, right):
        even = jnp.where(low, left, pltpu.roll(right, TILE, 1))
        odd = jnp.where(low, pltpu.roll(left, TILE, 1), right)
        return even.astype(jnp.bfloat16), odd.astype(jnp.bfloat16)

    def build_inward(n):
        for which, spread in enumerate((gate_t, up_t)):
            for row in range(row_tiles):
                both = join(tile_at(spread, n, row, 0), tile_at(spread, n, row, 1))
                for odd in range(2):
                    at = row * TILE + odd * pairs
                    inward_w[at : at + pairs, which * 128 : which * 128 + 128] = both[odd]

    def build_down(n, slot):
        for sub in range(2):
            for half in range(row_tiles // 2):
                both = join(
                    tile_at(down_t, n, 2 * half, sub), tile_at(down_t, n, 2 * half + 1, sub)
                )
                for odd in range(2):
                    at = sub * TILE + odd * pairs
                    down_w[slot, at : at + pairs, half * 128 : half * 128 + 128] = both[odd]

    def send(src, dst, send_sem, recv_sem, dp, tensor):
        return pltpu.make_async_remote_copy(
            src_ref=src, dst_ref=dst, send_sem=send_sem, recv_sem=recv_sem,
            device_id=(dp, tensor), device_id_type=MESH,
        )

    def slab(index):
        return pl.ds(pl.multiple_of(index * width, width), width)

    def head(d):
        to = (me + d) % n_dp
        return send(normed.at[:, slab(to)], xa.at[me], head_s.at[d], head_r.at[d], to, mt)

    def row(d):
        return send(xa, xg.at[mt], row_s.at[d], row_r.at[d], me, (mt + d) % n_tensor)

    for d in range(1, n_dp):
        head(d).start()
    xa[me] = normed[:, slab(me)]
    loads[0].wait()
    place_all(0, gate_t)
    for d in range(1, n_dp):
        head(d).wait_recv()
    for d in range(1, n_tensor):
        row(d).start()
    xg[mt] = xa[...]
    loads[1].wait()
    place_all(1, up_t)
    for d in range(1, n_tensor):
        row(d).wait_recv()
    tokens = n_tensor * n_dp * rows
    quarter = tokens // 4
    for at in range(0, width, 256):
        xp[:, at : at + 256] = jnp.dot(
            xg[:, :, :, at : at + 256].reshape(tokens, 256),
            order[...],
            preferred_element_type=jnp.float32,
        ).astype(jnp.bfloat16)
    acc[...] = jnp.zeros_like(acc)
    loads[2].wait()

    def pair_copy(n):
        return send(part.at[n, :, other], pair.at[n], pair_s.at[n], pair_r.at[n], buddy, mt)

    def chain_copy(n, h):
        return send(
            part.at[n, h, core], chain.at[n, h], chain_s.at[n, h], chain_r.at[n, h],
            jnp.clip(hops[h][1], 0, last) * 2 + core, mt,
        )

    def hid_copy(n, h):
        to = jnp.clip(hops[1 - h][1], 0, last) * 2 + core
        return send(
            hid.at[n, h, core], hid.at[n, h, core], hid_s.at[n, h], hid_r.at[n, h], to, mt
        )

    def core_copy(n, h):
        return send(
            hid.at[n, h, core], hid.at[n, h, core], core_s.at[n, h], core_r.at[n, h], buddy, mt
        )

    def project(n):
        build_inward(n)
        value = jnp.dot(xp[...], inward_w[...], preferred_element_type=jnp.float32)
        part[n] = value.astype(jnp.bfloat16).reshape(2, 2, quarter, 256)
        pair_copy(n).start()

    def inside(n):
        return (n >= 0) & (n < groups)

    ahead = 2
    for n in range(ahead):
        project(jnp.int32(n))
    nearest = jnp.minimum(z, last - z)
    farthest = jnp.maximum(z, last - z)

    def step(s, carry):
        @pl.when(inside(s - LAG * nearest))
        def _():
            pair_copy(s - LAG * nearest).wait_recv()

        for h in range(2):
            position = hops[h][0]
            n = s - LAG * position

            @pl.when(inside(n))
            def _():
                def own():
                    return part[n, h, core].astype(jnp.float32) + pair[n, h].astype(jnp.float32)

                @pl.when(position > 0)
                def _():
                    chain_copy(n, h).wait_recv()

                @pl.when(position == 0)
                def _():
                    part[n, h, core] = own().astype(jnp.bfloat16)

                @pl.when((position > 0) & (position < last))
                def _():
                    part[n, h, core] = (own() + chain[n, h].astype(jnp.float32)).astype(jnp.bfloat16)

                @pl.when(position < last)
                def _():
                    chain_copy(n, h).start()

                @pl.when(position == last)
                def _():
                    total = own() + chain[n, h].astype(jnp.float32)
                    gate = total[:, :128]
                    value = gate / (1.0 + jnp.exp(-gate)) * total[:, 128:]
                    hid[n, h, core] = jnp.dot(
                        value.astype(jnp.bfloat16), order[:128, :128], preferred_element_type=jnp.float32
                    ).astype(jnp.bfloat16)

        for h in range(2):
            distance = last - hops[h][0]
            n = s - LAG * (last + distance)

            @pl.when(inside(n))
            def _():
                @pl.when(distance > 0)
                def _():
                    hid_copy(n, h).wait_recv()

                @pl.when(distance < last)
                def _():
                    hid_copy(n, h).start()

                core_copy(n, h).start()

        @pl.when(s + ahead < groups)
        def _():
            project(s + ahead)

        @pl.when(s < TILE * TILE // WIDE)
        def _():
            place_tiles(2, down_t, s)

        done = s - LAG * (last + farthest) - 1

        @pl.when(inside(done))
        def _():
            for h in range(2):
                core_copy(done, h).wait_recv()
            build_down(done, done % 2)

            @pl.when(done % 2 == 1)
            def _():
                both = jnp.concatenate(
                    [hid[done - 1].reshape(tokens, 128), hid[done].reshape(tokens, 128)], axis=1
                )
                acc[...] += jnp.dot(
                    both, down_w[...].reshape(256, width), preferred_element_type=jnp.float32
                )

        return carry

    lax.fori_loop(0, groups + 2 * LAG * last + 1, step, 0)

    tail[...] = acc[...].astype(jnp.bfloat16).reshape(tail.shape)

    def tail_copy(d):
        to = (mt + d) % n_tensor
        return send(tail.at[to], tail_in.at[mt], tail_s.at[d], tail_r.at[d], me, to)

    def back_copy(d):
        to = (me + d) % n_dp
        return send(mixed.at[to], back.at[me], back_s.at[d], back_r.at[d], to, mt)

    for d in range(1, n_tensor):
        tail_copy(d).start()
    tail_in[mt] = tail[mt]
    for d in range(1, n_tensor):
        tail_copy(d).wait_recv()
    total = tail_in[0].astype(jnp.float32)
    for t in range(1, n_tensor):
        total += tail_in[t].astype(jnp.float32)
    mixed[...] = total.astype(jnp.bfloat16).reshape(mixed.shape)
    for d in range(1, n_dp):
        back_copy(d).start()
    back[me] = mixed[me]

    def drain(n, carry):
        pair_copy(n).wait_send()
        for h in range(2):
            core_copy(n, h).wait_send()

            @pl.when(hops[h][0] < last)
            def _():
                chain_copy(n, h).wait_send()

            @pl.when(last - hops[h][0] < last)
            def _():
                hid_copy(n, h).wait_send()

        return carry

    lax.fori_loop(0, groups, drain, 0)
    for d in range(1, n_dp):
        head(d).wait_send()
        back_copy(d).wait_recv()
        back_copy(d).wait_send()
    for d in range(1, n_tensor):
        row(d).wait_send()
        tail_copy(d).wait_send()
    for p in range(n_dp):
        out[:, p * width : p * width + width] = back[p]


def flow(tokens, gain, ids, counts, gate_p, up_p, down_p, n_dp, n_tensor, row_tiles, col_tiles):
    groups = col_tiles // 2
    width = row_tiles * TILE
    rows = tokens.shape[0]
    total = rows * n_dp * n_tensor
    quarter = total // 4
    tiles = row_tiles * col_tiles
    half = jnp.bfloat16
    dma = pltpu.SemaphoreType.DMA
    vmem = pl.BlockSpec(memory_space=pltpu.VMEM)
    return pl.pallas_call(
        lambda *refs: flow_kernel(n_dp, n_tensor, row_tiles, col_tiles, *refs),
        out_shape=jax.ShapeDtypeStruct(tokens.shape, half),
        in_specs=[vmem] * 3 + [pl.BlockSpec(memory_space=pltpu.SMEM)] + [pl.BlockSpec(memory_space=pl.ANY)] * 3,
        out_specs=vmem,
        scratch_shapes=[
            pltpu.VMEM(tokens.shape, half),
            pltpu.VMEM((256, 256), half),
            pltpu.VMEM((3,) + gate_p.shape, half),
            pltpu.VMEM((tiles * TILE // 2, 128), jnp.float32),
            pltpu.VMEM((tiles * TILE // 2, 128), jnp.float32),
            pltpu.VMEM((tiles * TILE // 2, 128), jnp.float32),
            pltpu.VMEM((width, 256), half),
            pltpu.VMEM((2, 128, width), half),
            pltpu.VMEM((n_dp, rows, width), half),
            pltpu.VMEM((n_tensor, n_dp, rows, width), half),
            pltpu.VMEM((total, width), half),
            pltpu.VMEM((groups, 2, 2, quarter, 256), half),
            pltpu.VMEM((groups, 2, quarter, 256), half),
            pltpu.VMEM((groups, 2, quarter, 256), half),
            pltpu.VMEM((groups, 2, 2, quarter, 128), half),
            pltpu.VMEM((total, width), jnp.float32),
            pltpu.VMEM((n_tensor, n_dp * rows, width), half),
            pltpu.VMEM((n_tensor, n_dp * rows, width), half),
            pltpu.VMEM((n_dp, rows, width), half),
            pltpu.VMEM((n_dp, rows, width), half),
            dma((3,)),
            dma((n_dp,)), dma((n_dp,)), dma((n_tensor,)), dma((n_tensor,)),
            dma((groups,)), dma((groups,)), dma((groups, 2)), dma((groups, 2)),
            dma((groups, 2)), dma((groups, 2)), dma((groups, 2)), dma((groups, 2)),
            dma((n_tensor,)), dma((n_tensor,)), dma((n_dp,)), dma((n_dp,)),
        ],
        compiler_params=pltpu.CompilerParams(
            collective_id=0, has_side_effects=True, vmem_limit_bytes=60 << 20
        ),
        cost_estimate=pl.CostEstimate(
            flops=9 * 10**9, bytes_accessed=6 << 20, transcendentals=10**6
        ),
        name="flow",
    )(tokens, gain, ids, counts, gate_p, up_p, down_p)


def local(tokens, norm_gain, gate_tiles, up_tiles, down_tiles, tile_ids, tile_counts):
    n_dp, n_tensor = lax.axis_size("dp"), lax.axis_size("tensor")
    row_tiles = D // (TILE * n_dp)
    col_tiles = FF // (TILE * n_tensor)
    if col_tiles % 8 != 0 or row_tiles % 4 != 0 or n_tensor != 4 or n_dp != 8:
        return local_plain(
            tokens, norm_gain, gate_tiles, up_tiles, down_tiles, tile_ids, tile_counts
        )
    return flow(
        tokens, norm_gain, tile_ids[0, 0][:, None, :], tile_counts,
        gate_tiles[0, 0], up_tiles[0, 0], down_tiles[0, 0],
        n_dp, n_tensor, row_tiles, col_tiles,
    )


def solution(mesh):
    return jax.shard_map(
        local,
        mesh=mesh,
        in_specs=(
            P(("dp", "tensor"), None),
            P(),
            P("tensor", "dp", None, None),
            P("tensor", "dp", None, None),
            P("tensor", "dp", None, None),
            P("tensor", "dp", None, None),
            P("tensor", "dp", None),
        ),
        out_specs=P(("dp", "tensor"), None),
        check_vma=False,
    )
```

```python
import jax
import jax.numpy as jnp
from jax import lax
from jax.experimental import pallas as pl
from jax.experimental.pallas import tpu as pltpu
from jax.sharding import PartitionSpec as P

D = 4096
FF = 14336
TILE = 64
MESH = pl.DeviceIdType.MESH


def normalize(values, norm_gain):
    wide = values.astype(jnp.float32)
    meansq = jnp.mean(wide * wide, axis=-1, keepdims=True)
    return (wide * lax.rsqrt(meansq + 1e-05) * norm_gain).astype(jnp.bfloat16)


def unpack_tiles(packed, slot_ids, counts, row_tiles, col_tiles):
    local_tiles = row_tiles * col_tiles
    slots = slot_ids.shape[0]
    active = jnp.arange(slots) < counts
    select = ((slot_ids[:, None] == jnp.arange(local_tiles)[None, :]) & active[:, None]).astype(
        jnp.bfloat16
    )
    placed = jnp.einsum("kl,ke->le", select, packed, preferred_element_type=jnp.float32).astype(
        jnp.bfloat16
    )
    return placed.reshape(row_tiles, col_tiles, TILE, TILE)


def inward_block(packed, slot_ids, counts, row_tiles, col_tiles):
    placed = unpack_tiles(packed, slot_ids, counts, row_tiles, col_tiles)
    return placed.transpose(0, 2, 1, 3).reshape(row_tiles * TILE, col_tiles * TILE)


def outward_block(packed, slot_ids, counts, row_tiles, col_tiles):
    placed = unpack_tiles(packed, slot_ids, counts, row_tiles, col_tiles)
    return placed.transpose(1, 2, 0, 3).reshape(col_tiles * TILE, row_tiles * TILE)


def gather_features(tokens, norm_gain):
    n_dp = lax.axis_size("dp")
    rows = tokens.shape[0]
    normed = normalize(tokens, norm_gain)
    mine = lax.all_to_all(
        normed.reshape(rows, n_dp, D // n_dp).transpose(1, 0, 2), "dp", 0, 0, tiled=True
    )
    mine = lax.all_gather(mine, "tensor", axis=1, tiled=True)
    return mine.reshape(n_dp * lax.axis_size("tensor") * rows, D // n_dp)


def spread_rows(part):
    part = lax.all_to_all(part.astype(jnp.bfloat16), "dp", 0, 1, tiled=True)
    return lax.psum_scatter(part, "tensor", scatter_dimension=0, tiled=True)


def swiglu(gate, upward):
    gate = gate.astype(jnp.float32)
    return (jax.nn.silu(gate) * upward.astype(jnp.float32)).astype(jnp.bfloat16)


def local_plain(tokens, norm_gain, gate_tiles, up_tiles, down_tiles, tile_ids, tile_counts):
    row_tiles = D // (TILE * lax.axis_size("dp"))
    col_tiles = FF // (TILE * lax.axis_size("tensor"))
    ids, counts = tile_ids[0, 0], tile_counts[0, 0]
    mine = gather_features(tokens, norm_gain)
    gate_block = inward_block(gate_tiles[0, 0], ids[0], counts[0], row_tiles, col_tiles)
    up_block = inward_block(up_tiles[0, 0], ids[1], counts[1], row_tiles, col_tiles)
    down_block = outward_block(down_tiles[0, 0], ids[2], counts[2], row_tiles, col_tiles)
    gate = jnp.dot(mine, gate_block, preferred_element_type=jnp.float32)
    gate = lax.psum_scatter(gate, "dp", scatter_dimension=0, tiled=True)
    upward = jnp.dot(mine, up_block, preferred_element_type=jnp.float32)
    upward = lax.psum_scatter(upward, "dp", scatter_dimension=0, tiled=True)
    hidden = lax.all_gather(swiglu(gate, upward), "dp", axis=0, tiled=True)
    return spread_rows(jnp.dot(hidden, down_block, preferred_element_type=jnp.float32))


LAG = 2
WIDE = 512


def flow_kernel(
    n_dp, n_tensor, row_tiles, col_tiles,
    tokens_in, gain, ids, counts, gate_p, up_p, down_p, out,
    normed, order, packed, gate_t, up_t, down_t, inward_w, down_w,
    xa, xg, xp, part, pair, chain, hid, acc, tail, tail_in, mixed, back, load_s,
    head_s, head_r, row_s, row_r, pair_s, pair_r, chain_s, chain_r,
    hid_s, hid_r, core_s, core_r, tail_s, tail_r, back_s, back_r,
):
    me, mt = lax.axis_index("dp"), lax.axis_index("tensor")
    z, core = me // 2, me % 2
    chips = n_dp // 2
    last = chips - 1
    groups = part.shape[0]
    rows, width = xa.shape[1], xa.shape[2]
    other = 1 - core
    buddy = z * 2 + other
    hops = ((last - z, z - 1), (z, z + 1))

    barrier = pltpu.get_barrier_semaphore()
    for d in range(1, n_dp):
        pl.semaphore_signal(
            barrier, inc=1, device_id=((me + d) % n_dp, mt), device_id_type=MESH
        )
    for d in range(1, n_tensor):
        pl.semaphore_signal(
            barrier, inc=1, device_id=(me, (mt + d) % n_tensor), device_id_type=MESH
        )
    loads = [
        pltpu.make_async_copy(source, packed.at[i], load_s.at[i])
        for i, source in enumerate((gate_p, up_p, down_p))
    ]
    for load in loads:
        load.start()

    wide = tokens_in[...].astype(jnp.float32)
    meansq = jnp.mean(wide * wide, axis=-1, keepdims=True)
    normed[...] = (wide * lax.rsqrt(meansq + 1e-05) * gain[...].reshape(1, D)).astype(jnp.bfloat16)
    source = lax.broadcasted_iota(jnp.int32, (256, 256), 0)
    place = lax.broadcasted_iota(jnp.int32, (256, 256), 1)
    inner = place & (TILE - 1)
    wanted = place - inner + 2 * (inner & (TILE // 2 - 1)) + (inner >> 5)
    order[...] = (source == wanted).astype(jnp.bfloat16)
    pl.semaphore_wait(barrier, n_dp + n_tensor - 2)

    pairs = TILE // 2
    blocks = col_tiles // 8
    tiles = row_tiles * col_tiles
    slots = packed.shape[1]
    low = lax.broadcasted_iota(jnp.int32, (pairs, 128), 1) < TILE

    def place_tiles(which, spread, at):
        tile = lax.broadcasted_iota(jnp.int32, (tiles, slots), 0)
        slot = lax.broadcasted_iota(jnp.int32, (tiles, slots), 1)
        hit = (tile == ids[which]) & (slot < counts[0, 0, which])
        columns = pl.ds(pl.multiple_of(at * WIDE, WIDE), WIDE)
        placed = jnp.dot(
            hit.astype(jnp.bfloat16), packed[which, :, columns], preferred_element_type=jnp.float32
        )
        for sub in range(WIDE // 128):
            for block in range(tiles // 8):
                start = block * pairs * 8 + (at * (WIDE // 128) + sub) * 8
                spread[pl.ds(pl.multiple_of(start, 8), 8), :] = placed[
                    block * 8 : block * 8 + 8, sub * 128 : sub * 128 + 128
                ]

    def place_all(which, spread):
        def body(at, carry):
            place_tiles(which, spread, at)
            return carry

        lax.fori_loop(0, TILE * TILE // WIDE, body, 0)

    def tile_at(spread, n, row, sub):
        start = (row * blocks + n // 4) * pairs * 8 + (n % 4) * 2 + sub
        return spread[pl.ds(start, pairs, stride=8), :]

    def join(left, right):
        even = jnp.where(low, left, pltpu.roll(right, TILE, 1))
        odd = jnp.where(low, pltpu.roll(left, TILE, 1), right)
        return even.astype(jnp.bfloat16), odd.astype(jnp.bfloat16)

    def build_inward(n):
        for which, spread in enumerate((gate_t, up_t)):
            for row in range(row_tiles):
                both = join(tile_at(spread, n, row, 0), tile_at(spread, n, row, 1))
                for odd in range(2):
                    at = row * TILE + odd * pairs
                    inward_w[at : at + pairs, which * 128 : which * 128 + 128] = both[odd]

    def build_down(n, slot):
        for sub in range(2):
            for half in range(row_tiles // 2):
                both = join(
                    tile_at(down_t, n, 2 * half, sub), tile_at(down_t, n, 2 * half + 1, sub)
                )
                for odd in range(2):
                    at = sub * TILE + odd * pairs
                    down_w[slot, at : at + pairs, half * 128 : half * 128 + 128] = both[odd]

    def send(src, dst, send_sem, recv_sem, dp, tensor):
        return pltpu.make_async_remote_copy(
            src_ref=src, dst_ref=dst, send_sem=send_sem, recv_sem=recv_sem,
            device_id=(dp, tensor), device_id_type=MESH,
        )

    def slab(index):
        return pl.ds(pl.multiple_of(index * width, width), width)

    def head(d):
        to = (me + d) % n_dp
        return send(normed.at[:, slab(to)], xa.at[me], head_s.at[d], head_r.at[d], to, mt)

    def row(d):
        return send(xa, xg.at[mt], row_s.at[d], row_r.at[d], me, (mt + d) % n_tensor)

    for d in range(1, n_dp):
        head(d).start()
    xa[me] = normed[:, slab(me)]
    loads[0].wait()
    place_all(0, gate_t)
    for d in range(1, n_dp):
        head(d).wait_recv()
    for d in range(1, n_tensor):
        row(d).start()
    xg[mt] = xa[...]
    loads[1].wait()
    place_all(1, up_t)
    loads[2].wait()
    place_all(2, down_t)
    acc[...] = jnp.zeros_like(acc)
    for d in range(1, n_tensor):
        row(d).wait_recv()
    tokens = n_tensor * n_dp * rows
    quarter = tokens // 4
    for at in range(0, width, 256):
        xp[:, at : at + 256] = jnp.dot(
            xg[:, :, :, at : at + 256].reshape(tokens, 256),
            order[...],
            preferred_element_type=jnp.float32,
        ).astype(jnp.bfloat16)

    def pair_copy(n):
        return send(part.at[n, :, other], pair.at[n], pair_s.at[n], pair_r.at[n], buddy, mt)

    def chain_copy(n, h):
        return send(
            part.at[n, h, core], chain.at[n, h], chain_s.at[n, h], chain_r.at[n, h],
            jnp.clip(hops[h][1], 0, last) * 2 + core, mt,
        )

    def hid_copy(n, h):
        to = jnp.clip(hops[1 - h][1], 0, last) * 2 + core
        return send(
            hid.at[n, h, core], hid.at[n, h, core], hid_s.at[n, h], hid_r.at[n, h], to, mt
        )

    def core_copy(n, h):
        return send(
            hid.at[n, h, core], hid.at[n, h, core], core_s.at[n, h], core_r.at[n, h], buddy, mt
        )

    def project(n):
        build_inward(n)
        value = jnp.dot(xp[...], inward_w[...], preferred_element_type=jnp.float32)
        part[n] = value.astype(jnp.bfloat16).reshape(2, 2, quarter, 256)
        pair_copy(n).start()

    def inside(n):
        return (n >= 0) & (n < groups)

    ahead = 2
    for n in range(ahead):
        project(jnp.int32(n))
    nearest = jnp.minimum(z, last - z)
    farthest = jnp.maximum(z, last - z)

    def step(s, carry):
        @pl.when(inside(s - LAG * nearest))
        def _():
            pair_copy(s - LAG * nearest).wait_recv()

        for h in range(2):
            position = hops[h][0]
            n = s - LAG * position

            @pl.when(inside(n))
            def _():
                def own():
                    return part[n, h, core].astype(jnp.float32) + pair[n, h].astype(jnp.float32)

                @pl.when(position > 0)
                def _():
                    chain_copy(n, h).wait_recv()

                @pl.when(position == 0)
                def _():
                    part[n, h, core] = own().astype(jnp.bfloat16)

                @pl.when((position > 0) & (position < last))
                def _():
                    part[n, h, core] = (own() + chain[n, h].astype(jnp.float32)).astype(jnp.bfloat16)

                @pl.when(position < last)
                def _():
                    chain_copy(n, h).start()

                @pl.when(position == last)
                def _():
                    total = own() + chain[n, h].astype(jnp.float32)
                    gate = total[:, :128]
                    value = gate / (1.0 + jnp.exp(-gate)) * total[:, 128:]
                    hid[n, h, core] = jnp.dot(
                        value.astype(jnp.bfloat16), order[:128, :128], preferred_element_type=jnp.float32
                    ).astype(jnp.bfloat16)

        for h in range(2):
            distance = last - hops[h][0]
            n = s - LAG * (last + distance)

            @pl.when(inside(n))
            def _():
                @pl.when(distance > 0)
                def _():
                    hid_copy(n, h).wait_recv()

                @pl.when(distance < last)
                def _():
                    hid_copy(n, h).start()

                core_copy(n, h).start()

        @pl.when(s + ahead < groups)
        def _():
            project(s + ahead)

        done = s - LAG * (last + farthest) - 1

        @pl.when(inside(done))
        def _():
            for h in range(2):
                core_copy(done, h).wait_recv()
            build_down(done, done % 2)

            @pl.when(done % 2 == 1)
            def _():
                both = jnp.concatenate(
                    [hid[done - 1].reshape(tokens, 128), hid[done].reshape(tokens, 128)], axis=1
                )
                acc[...] += jnp.dot(
                    both, down_w[...].reshape(256, width), preferred_element_type=jnp.float32
                )

        return carry

    lax.fori_loop(0, groups + 2 * LAG * last + 1, step, 0)

    tail[...] = acc[...].astype(jnp.bfloat16).reshape(tail.shape)

    def tail_copy(d):
        to = (mt + d) % n_tensor
        return send(tail.at[to], tail_in.at[mt], tail_s.at[d], tail_r.at[d], me, to)

    def back_copy(d):
        to = (me + d) % n_dp
        return send(mixed.at[to], back.at[me], back_s.at[d], back_r.at[d], to, mt)

    for d in range(1, n_tensor):
        tail_copy(d).start()
    tail_in[mt] = tail[mt]

    def drain(n, carry):
        pair_copy(n).wait_send()
        for h in range(2):
            core_copy(n, h).wait_send()

            @pl.when(hops[h][0] < last)
            def _():
                chain_copy(n, h).wait_send()

            @pl.when(last - hops[h][0] < last)
            def _():
                hid_copy(n, h).wait_send()

        return carry

    lax.fori_loop(0, groups, drain, 0)
    for d in range(1, n_dp):
        head(d).wait_send()
    for d in range(1, n_tensor):
        row(d).wait_send()
    for d in range(1, n_tensor):
        tail_copy(d).wait_recv()
    total = tail_in[0].astype(jnp.float32)
    for t in range(1, n_tensor):
        total += tail_in[t].astype(jnp.float32)
    mixed[...] = total.astype(jnp.bfloat16).reshape(mixed.shape)
    for d in range(1, n_dp):
        back_copy(d).start()
    back[me] = mixed[me]

    for d in range(1, n_dp):
        back_copy(d).wait_recv()
        back_copy(d).wait_send()
    for d in range(1, n_tensor):
        tail_copy(d).wait_send()
    for p in range(n_dp):
        out[:, p * width : p * width + width] = back[p]


def flow(tokens, gain, ids, counts, gate_p, up_p, down_p, n_dp, n_tensor, row_tiles, col_tiles):
    groups = col_tiles // 2
    width = row_tiles * TILE
    rows = tokens.shape[0]
    total = rows * n_dp * n_tensor
    quarter = total // 4
    tiles = row_tiles * col_tiles
    half = jnp.bfloat16
    dma = pltpu.SemaphoreType.DMA
    vmem = pl.BlockSpec(memory_space=pltpu.VMEM)
    return pl.pallas_call(
        lambda *refs: flow_kernel(n_dp, n_tensor, row_tiles, col_tiles, *refs),
        out_shape=jax.ShapeDtypeStruct(tokens.shape, half),
        in_specs=[vmem] * 3 + [pl.BlockSpec(memory_space=pltpu.SMEM)] + [pl.BlockSpec(memory_space=pl.ANY)] * 3,
        out_specs=vmem,
        scratch_shapes=[
            pltpu.VMEM(tokens.shape, half),
            pltpu.VMEM((256, 256), half),
            pltpu.VMEM((3,) + gate_p.shape, half),
            pltpu.VMEM((tiles * TILE // 2, 128), jnp.float32),
            pltpu.VMEM((tiles * TILE // 2, 128), jnp.float32),
            pltpu.VMEM((tiles * TILE // 2, 128), jnp.float32),
            pltpu.VMEM((width, 256), half),
            pltpu.VMEM((2, 128, width), half),
            pltpu.VMEM((n_dp, rows, width), half),
            pltpu.VMEM((n_tensor, n_dp, rows, width), half),
            pltpu.VMEM((total, width), half),
            pltpu.VMEM((groups, 2, 2, quarter, 256), half),
            pltpu.VMEM((groups, 2, quarter, 256), half),
            pltpu.VMEM((groups, 2, quarter, 256), half),
            pltpu.VMEM((groups, 2, 2, quarter, 128), half),
            pltpu.VMEM((total, width), jnp.float32),
            pltpu.VMEM((n_tensor, n_dp * rows, width), half),
            pltpu.VMEM((n_tensor, n_dp * rows, width), half),
            pltpu.VMEM((n_dp, rows, width), half),
            pltpu.VMEM((n_dp, rows, width), half),
            dma((3,)),
            dma((n_dp,)), dma((n_dp,)), dma((n_tensor,)), dma((n_tensor,)),
            dma((groups,)), dma((groups,)), dma((groups, 2)), dma((groups, 2)),
            dma((groups, 2)), dma((groups, 2)), dma((groups, 2)), dma((groups, 2)),
            dma((n_tensor,)), dma((n_tensor,)), dma((n_dp,)), dma((n_dp,)),
        ],
        compiler_params=pltpu.CompilerParams(
            collective_id=0, has_side_effects=True, vmem_limit_bytes=60 << 20
        ),
        cost_estimate=pl.CostEstimate(
            flops=9 * 10**9, bytes_accessed=6 << 20, transcendentals=10**6
        ),
        name="flow",
    )(tokens, gain, ids, counts, gate_p, up_p, down_p)


def local(tokens, norm_gain, gate_tiles, up_tiles, down_tiles, tile_ids, tile_counts):
    n_dp, n_tensor = lax.axis_size("dp"), lax.axis_size("tensor")
    row_tiles = D // (TILE * n_dp)
    col_tiles = FF // (TILE * n_tensor)
    if col_tiles % 8 != 0 or row_tiles % 4 != 0 or n_tensor != 4 or n_dp != 8:
        return local_plain(
            tokens, norm_gain, gate_tiles, up_tiles, down_tiles, tile_ids, tile_counts
        )
    return flow(
        tokens, norm_gain, tile_ids[0, 0][:, None, :], tile_counts,
        gate_tiles[0, 0], up_tiles[0, 0], down_tiles[0, 0],
        n_dp, n_tensor, row_tiles, col_tiles,
    )


def solution(mesh):
    return jax.shard_map(
        local,
        mesh=mesh,
        in_specs=(
            P(("dp", "tensor"), None),
            P(),
            P("tensor", "dp", None, None),
            P("tensor", "dp", None, None),
            P("tensor", "dp", None, None),
            P("tensor", "dp", None, None),
            P("tensor", "dp", None),
        ),
        out_specs=P(("dp", "tensor"), None),
        check_vma=False,
    )
```

```python
import jax
import jax.numpy as jnp
from jax import lax
from jax.experimental import pallas as pl
from jax.experimental.pallas import tpu as pltpu
from jax.sharding import PartitionSpec as P

D = 4096
FF = 14336
TILE = 64
MESH = pl.DeviceIdType.MESH


def normalize(values, norm_gain):
    wide = values.astype(jnp.float32)
    meansq = jnp.mean(wide * wide, axis=-1, keepdims=True)
    return (wide * lax.rsqrt(meansq + 1e-05) * norm_gain).astype(jnp.bfloat16)


def unpack_tiles(packed, slot_ids, counts, row_tiles, col_tiles):
    local_tiles = row_tiles * col_tiles
    slots = slot_ids.shape[0]
    active = jnp.arange(slots) < counts
    select = ((slot_ids[:, None] == jnp.arange(local_tiles)[None, :]) & active[:, None]).astype(
        jnp.bfloat16
    )
    placed = jnp.einsum("kl,ke->le", select, packed, preferred_element_type=jnp.float32).astype(
        jnp.bfloat16
    )
    return placed.reshape(row_tiles, col_tiles, TILE, TILE)


def inward_block(packed, slot_ids, counts, row_tiles, col_tiles):
    placed = unpack_tiles(packed, slot_ids, counts, row_tiles, col_tiles)
    return placed.transpose(0, 2, 1, 3).reshape(row_tiles * TILE, col_tiles * TILE)


def outward_block(packed, slot_ids, counts, row_tiles, col_tiles):
    placed = unpack_tiles(packed, slot_ids, counts, row_tiles, col_tiles)
    return placed.transpose(1, 2, 0, 3).reshape(col_tiles * TILE, row_tiles * TILE)


def gather_features(tokens, norm_gain):
    n_dp = lax.axis_size("dp")
    rows = tokens.shape[0]
    normed = normalize(tokens, norm_gain)
    mine = lax.all_to_all(
        normed.reshape(rows, n_dp, D // n_dp).transpose(1, 0, 2), "dp", 0, 0, tiled=True
    )
    mine = lax.all_gather(mine, "tensor", axis=1, tiled=True)
    return mine.reshape(n_dp * lax.axis_size("tensor") * rows, D // n_dp)


def spread_rows(part):
    part = lax.all_to_all(part.astype(jnp.bfloat16), "dp", 0, 1, tiled=True)
    return lax.psum_scatter(part, "tensor", scatter_dimension=0, tiled=True)


def swiglu(gate, upward):
    gate = gate.astype(jnp.float32)
    return (jax.nn.silu(gate) * upward.astype(jnp.float32)).astype(jnp.bfloat16)


def local_plain(tokens, norm_gain, gate_tiles, up_tiles, down_tiles, tile_ids, tile_counts):
    row_tiles = D // (TILE * lax.axis_size("dp"))
    col_tiles = FF // (TILE * lax.axis_size("tensor"))
    ids, counts = tile_ids[0, 0], tile_counts[0, 0]
    mine = gather_features(tokens, norm_gain)
    gate_block = inward_block(gate_tiles[0, 0], ids[0], counts[0], row_tiles, col_tiles)
    up_block = inward_block(up_tiles[0, 0], ids[1], counts[1], row_tiles, col_tiles)
    down_block = outward_block(down_tiles[0, 0], ids[2], counts[2], row_tiles, col_tiles)
    gate = jnp.dot(mine, gate_block, preferred_element_type=jnp.float32)
    gate = lax.psum_scatter(gate, "dp", scatter_dimension=0, tiled=True)
    upward = jnp.dot(mine, up_block, preferred_element_type=jnp.float32)
    upward = lax.psum_scatter(upward, "dp", scatter_dimension=0, tiled=True)
    hidden = lax.all_gather(swiglu(gate, upward), "dp", axis=0, tiled=True)
    return spread_rows(jnp.dot(hidden, down_block, preferred_element_type=jnp.float32))


LAG = 2
WIDE = 512


def flow_kernel(
    n_dp, n_tensor, row_tiles, col_tiles,
    tokens_in, gain, ids, counts, gate_p, up_p, down_p, out,
    normed, order, packed, gate_t, up_t, down_t, inward_w, down_w,
    xa, xg, xp, part, pair, chain, hid, acc, tail, tail_in, mixed, back, load_s,
    head_s, head_r, row_s, row_r, pair_s, pair_r, chain_s, chain_r,
    hid_s, hid_r, core_s, core_r, tail_s, tail_r, back_s, back_r,
):
    me, mt = lax.axis_index("dp"), lax.axis_index("tensor")
    z, core = me // 2, me % 2
    chips = n_dp // 2
    last = chips - 1
    groups = part.shape[0]
    rows, width = xa.shape[1], xa.shape[2]
    other = 1 - core
    buddy = z * 2 + other
    hops = ((last - z, z - 1), (z, z + 1))

    barrier = pltpu.get_barrier_semaphore()
    for d in range(1, n_dp):
        pl.semaphore_signal(
            barrier, inc=1, device_id=((me + d) % n_dp, mt), device_id_type=MESH
        )
    for d in range(1, n_tensor):
        pl.semaphore_signal(
            barrier, inc=1, device_id=(me, (mt + d) % n_tensor), device_id_type=MESH
        )
    loads = [
        pltpu.make_async_copy(source, packed.at[i], load_s.at[i])
        for i, source in enumerate((gate_p, up_p, down_p))
    ]
    for load in loads:
        load.start()

    wide = tokens_in[...].astype(jnp.float32)
    meansq = jnp.mean(wide * wide, axis=-1, keepdims=True)
    normed[...] = (wide * lax.rsqrt(meansq + 1e-05) * gain[...].reshape(1, D)).astype(jnp.bfloat16)
    source = lax.broadcasted_iota(jnp.int32, (256, 256), 0)
    place = lax.broadcasted_iota(jnp.int32, (256, 256), 1)
    inner = place & (TILE - 1)
    wanted = place - inner + 2 * (inner & (TILE // 2 - 1)) + (inner >> 5)
    order[...] = (source == wanted).astype(jnp.bfloat16)
    pl.semaphore_wait(barrier, n_dp + n_tensor - 2)

    pairs = TILE // 2
    blocks = col_tiles // 8
    tiles = row_tiles * col_tiles
    slots = packed.shape[1]
    low = lax.broadcasted_iota(jnp.int32, (pairs, 128), 1) < TILE

    def place_tiles(which, spread, at):
        tile = lax.broadcasted_iota(jnp.int32, (tiles, slots), 0)
        slot = lax.broadcasted_iota(jnp.int32, (tiles, slots), 1)
        hit = (tile == ids[which]) & (slot < counts[0, 0, which])
        columns = pl.ds(pl.multiple_of(at * WIDE, WIDE), WIDE)
        placed = jnp.dot(
            hit.astype(jnp.bfloat16), packed[which, :, columns], preferred_element_type=jnp.float32
        )
        for sub in range(WIDE // 128):
            for block in range(tiles // 8):
                start = block * pairs * 8 + (at * (WIDE // 128) + sub) * 8
                spread[pl.ds(pl.multiple_of(start, 8), 8), :] = placed[
                    block * 8 : block * 8 + 8, sub * 128 : sub * 128 + 128
                ]

    def place_all(which, spread):
        def body(at, carry):
            place_tiles(which, spread, at)
            return carry

        lax.fori_loop(0, TILE * TILE // WIDE, body, 0)

    def tile_at(spread, n, row, sub):
        start = (row * blocks + n // 4) * pairs * 8 + (n % 4) * 2 + sub
        return spread[pl.ds(start, pairs, stride=8), :]

    def join(left, right):
        even = jnp.where(low, left, pltpu.roll(right, TILE, 1))
        odd = jnp.where(low, pltpu.roll(left, TILE, 1), right)
        return even.astype(jnp.bfloat16), odd.astype(jnp.bfloat16)

    def build_inward(n):
        for which, spread in enumerate((gate_t, up_t)):
            for row in range(row_tiles):
                both = join(tile_at(spread, n, row, 0), tile_at(spread, n, row, 1))
                for odd in range(2):
                    at = row * TILE + odd * pairs
                    inward_w[at : at + pairs, which * 128 : which * 128 + 128] = both[odd]

    def build_down(n, slot):
        for sub in range(2):
            for half in range(row_tiles // 2):
                both = join(
                    tile_at(down_t, n, 2 * half, sub), tile_at(down_t, n, 2 * half + 1, sub)
                )
                for odd in range(2):
                    at = sub * TILE + odd * pairs
                    down_w[slot, at : at + pairs, half * 128 : half * 128 + 128] = both[odd]

    def send(src, dst, send_sem, recv_sem, dp, tensor):
        return pltpu.make_async_remote_copy(
            src_ref=src, dst_ref=dst, send_sem=send_sem, recv_sem=recv_sem,
            device_id=(dp, tensor), device_id_type=MESH,
        )

    def slab(index):
        return pl.ds(pl.multiple_of(index * width, width), width)

    def head(d):
        to = (me + d) % n_dp
        return send(normed.at[:, slab(to)], xa.at[me], head_s.at[d], head_r.at[d], to, mt)

    def row(d):
        return send(xa, xg.at[mt], row_s.at[d], row_r.at[d], me, (mt + d) % n_tensor)

    for d in range(1, n_dp):
        head(d).start()
    xa[me] = normed[:, slab(me)]
    loads[0].wait()
    place_all(0, gate_t)
    for d in range(1, n_dp):
        head(d).wait_recv()
    for d in range(1, n_tensor):
        row(d).start()
    xg[mt] = xa[...]
    loads[1].wait()
    place_all(1, up_t)
    loads[2].wait()
    place_all(2, down_t)
    acc[...] = jnp.zeros_like(acc)
    for d in range(1, n_tensor):
        row(d).wait_recv()
    tokens = n_tensor * n_dp * rows
    quarter = tokens // 4
    for at in range(0, width, 256):
        xp[:, at : at + 256] = jnp.dot(
            xg[:, :, :, at : at + 256].reshape(tokens, 256),
            order[...],
            preferred_element_type=jnp.float32,
        ).astype(jnp.bfloat16)

    def pair_copy(n):
        return send(part.at[n, :, other], pair.at[n], pair_s.at[n], pair_r.at[n], buddy, mt)

    def chain_copy(n, h):
        return send(
            part.at[n, h, core], chain.at[n, h], chain_s.at[n, h], chain_r.at[n, h],
            jnp.clip(hops[h][1], 0, last) * 2 + core, mt,
        )

    def hid_copy(n, h):
        to = jnp.clip(hops[1 - h][1], 0, last) * 2 + core
        return send(
            hid.at[n, h, core], hid.at[n, h, core], hid_s.at[n, h], hid_r.at[n, h], to, mt
        )

    def core_copy(n, h):
        return send(
            hid.at[n, h, core], hid.at[n, h, core], core_s.at[n, h], core_r.at[n, h], buddy, mt
        )

    def project(n):
        build_inward(n)
        value = jnp.dot(xp[...], inward_w[...], preferred_element_type=jnp.float32)
        part[n] = value.astype(jnp.bfloat16).reshape(2, 2, quarter, 256)
        pair_copy(n).start()

    def inside(n):
        return (n >= 0) & (n < groups)

    ahead = 2
    for n in range(ahead):
        project(jnp.int32(n))
    nearest = jnp.minimum(z, last - z)
    farthest = jnp.maximum(z, last - z)

    def step(s, carry):
        for h in range(2):
            distance = last - hops[h][0]
            n = s - LAG * last - 1 - distance

            @pl.when(inside(n))
            def _():
                @pl.when(distance > 0)
                def _():
                    hid_copy(n, h).wait_recv()

                @pl.when(distance < last)
                def _():
                    hid_copy(n, h).start()

                core_copy(n, h).start()

        @pl.when(inside(s - LAG * nearest))
        def _():
            pair_copy(s - LAG * nearest).wait_recv()

        for h in range(2):
            position = hops[h][0]
            n = s - LAG * position

            @pl.when(inside(n))
            def _():
                def own():
                    return part[n, h, core].astype(jnp.float32) + pair[n, h].astype(jnp.float32)

                @pl.when(position > 0)
                def _():
                    chain_copy(n, h).wait_recv()

                @pl.when(position == 0)
                def _():
                    part[n, h, core] = own().astype(jnp.bfloat16)

                @pl.when((position > 0) & (position < last))
                def _():
                    part[n, h, core] = (own() + chain[n, h].astype(jnp.float32)).astype(jnp.bfloat16)

                @pl.when(position < last)
                def _():
                    chain_copy(n, h).start()

                @pl.when(position == last)
                def _():
                    total = own() + chain[n, h].astype(jnp.float32)
                    gate = total[:, :128]
                    value = gate / (1.0 + jnp.exp(-gate)) * total[:, 128:]
                    hid[n, h, core] = jnp.dot(
                        value.astype(jnp.bfloat16), order[:128, :128], preferred_element_type=jnp.float32
                    ).astype(jnp.bfloat16)

        @pl.when(s + ahead < groups)
        def _():
            project(s + ahead)

        done = s - LAG * last - farthest - 2

        @pl.when(inside(done))
        def _():
            for h in range(2):
                core_copy(done, h).wait_recv()
            build_down(done, done % 2)

            @pl.when(done % 2 == 1)
            def _():
                both = jnp.concatenate(
                    [hid[done - 1].reshape(tokens, 128), hid[done].reshape(tokens, 128)], axis=1
                )
                acc[...] += jnp.dot(
                    both, down_w[...].reshape(256, width), preferred_element_type=jnp.float32
                )

        return carry

    lax.fori_loop(0, groups + LAG * last + last + 2, step, 0)

    tail[...] = acc[...].astype(jnp.bfloat16).reshape(tail.shape)

    def tail_copy(d):
        to = (mt + d) % n_tensor
        return send(tail.at[to], tail_in.at[mt], tail_s.at[d], tail_r.at[d], me, to)

    def back_copy(d):
        to = (me + d) % n_dp
        return send(mixed.at[to], back.at[me], back_s.at[d], back_r.at[d], to, mt)

    for d in range(1, n_tensor):
        tail_copy(d).start()
    tail_in[mt] = tail[mt]

    def drain(n, carry):
        pair_copy(n).wait_send()
        for h in range(2):
            core_copy(n, h).wait_send()

            @pl.when(hops[h][0] < last)
            def _():
                chain_copy(n, h).wait_send()

            @pl.when(last - hops[h][0] < last)
            def _():
                hid_copy(n, h).wait_send()

        return carry

    lax.fori_loop(0, groups, drain, 0)
    for d in range(1, n_dp):
        head(d).wait_send()
    for d in range(1, n_tensor):
        row(d).wait_send()
    for d in range(1, n_tensor):
        tail_copy(d).wait_recv()
    total = tail_in[0].astype(jnp.float32)
    for t in range(1, n_tensor):
        total += tail_in[t].astype(jnp.float32)
    mixed[...] = total.astype(jnp.bfloat16).reshape(mixed.shape)
    for d in range(1, n_dp):
        back_copy(d).start()
    back[me] = mixed[me]

    for d in range(1, n_dp):
        back_copy(d).wait_recv()
        back_copy(d).wait_send()
    for d in range(1, n_tensor):
        tail_copy(d).wait_send()
    for p in range(n_dp):
        out[:, p * width : p * width + width] = back[p]


def flow(tokens, gain, ids, counts, gate_p, up_p, down_p, n_dp, n_tensor, row_tiles, col_tiles):
    groups = col_tiles // 2
    width = row_tiles * TILE
    rows = tokens.shape[0]
    total = rows * n_dp * n_tensor
    quarter = total // 4
    tiles = row_tiles * col_tiles
    half = jnp.bfloat16
    dma = pltpu.SemaphoreType.DMA
    vmem = pl.BlockSpec(memory_space=pltpu.VMEM)
    return pl.pallas_call(
        lambda *refs: flow_kernel(n_dp, n_tensor, row_tiles, col_tiles, *refs),
        out_shape=jax.ShapeDtypeStruct(tokens.shape, half),
        in_specs=[vmem] * 3 + [pl.BlockSpec(memory_space=pltpu.SMEM)] + [pl.BlockSpec(memory_space=pl.ANY)] * 3,
        out_specs=vmem,
        scratch_shapes=[
            pltpu.VMEM(tokens.shape, half),
            pltpu.VMEM((256, 256), half),
            pltpu.VMEM((3,) + gate_p.shape, half),
            pltpu.VMEM((tiles * TILE // 2, 128), jnp.float32),
            pltpu.VMEM((tiles * TILE // 2, 128), jnp.float32),
            pltpu.VMEM((tiles * TILE // 2, 128), jnp.float32),
            pltpu.VMEM((width, 256), half),
            pltpu.VMEM((2, 128, width), half),
            pltpu.VMEM((n_dp, rows, width), half),
            pltpu.VMEM((n_tensor, n_dp, rows, width), half),
            pltpu.VMEM((total, width), half),
            pltpu.VMEM((groups, 2, 2, quarter, 256), half),
            pltpu.VMEM((groups, 2, quarter, 256), half),
            pltpu.VMEM((groups, 2, quarter, 256), half),
            pltpu.VMEM((groups, 2, 2, quarter, 128), half),
            pltpu.VMEM((total, width), jnp.float32),
            pltpu.VMEM((n_tensor, n_dp * rows, width), half),
            pltpu.VMEM((n_tensor, n_dp * rows, width), half),
            pltpu.VMEM((n_dp, rows, width), half),
            pltpu.VMEM((n_dp, rows, width), half),
            dma((3,)),
            dma((n_dp,)), dma((n_dp,)), dma((n_tensor,)), dma((n_tensor,)),
            dma((groups,)), dma((groups,)), dma((groups, 2)), dma((groups, 2)),
            dma((groups, 2)), dma((groups, 2)), dma((groups, 2)), dma((groups, 2)),
            dma((n_tensor,)), dma((n_tensor,)), dma((n_dp,)), dma((n_dp,)),
        ],
        compiler_params=pltpu.CompilerParams(
            collective_id=0, has_side_effects=True, vmem_limit_bytes=60 << 20
        ),
        cost_estimate=pl.CostEstimate(
            flops=9 * 10**9, bytes_accessed=6 << 20, transcendentals=10**6
        ),
        name="flow",
    )(tokens, gain, ids, counts, gate_p, up_p, down_p)


def local(tokens, norm_gain, gate_tiles, up_tiles, down_tiles, tile_ids, tile_counts):
    n_dp, n_tensor = lax.axis_size("dp"), lax.axis_size("tensor")
    row_tiles = D // (TILE * n_dp)
    col_tiles = FF // (TILE * n_tensor)
    if col_tiles % 8 != 0 or row_tiles % 4 != 0 or n_tensor != 4 or n_dp != 8:
        return local_plain(
            tokens, norm_gain, gate_tiles, up_tiles, down_tiles, tile_ids, tile_counts
        )
    return flow(
        tokens, norm_gain, tile_ids[0, 0][:, None, :], tile_counts,
        gate_tiles[0, 0], up_tiles[0, 0], down_tiles[0, 0],
        n_dp, n_tensor, row_tiles, col_tiles,
    )


def solution(mesh):
    return jax.shard_map(
        local,
        mesh=mesh,
        in_specs=(
            P(("dp", "tensor"), None),
            P(),
            P("tensor", "dp", None, None),
            P("tensor", "dp", None, None),
            P("tensor", "dp", None, None),
            P("tensor", "dp", None, None),
            P("tensor", "dp", None),
        ),
        out_specs=P(("dp", "tensor"), None),
        check_vma=False,
    )
```

```python
import jax
import jax.numpy as jnp
from jax import lax
from jax.experimental import pallas as pl
from jax.experimental.pallas import tpu as pltpu
from jax.sharding import PartitionSpec as P

D = 4096
FF = 14336
TILE = 64
MESH = pl.DeviceIdType.MESH


def normalize(values, norm_gain):
    wide = values.astype(jnp.float32)
    meansq = jnp.mean(wide * wide, axis=-1, keepdims=True)
    return (wide * lax.rsqrt(meansq + 1e-05) * norm_gain).astype(jnp.bfloat16)


def unpack_tiles(packed, slot_ids, counts, row_tiles, col_tiles):
    local_tiles = row_tiles * col_tiles
    slots = slot_ids.shape[0]
    active = jnp.arange(slots) < counts
    select = ((slot_ids[:, None] == jnp.arange(local_tiles)[None, :]) & active[:, None]).astype(
        jnp.bfloat16
    )
    placed = jnp.einsum("kl,ke->le", select, packed, preferred_element_type=jnp.float32).astype(
        jnp.bfloat16
    )
    return placed.reshape(row_tiles, col_tiles, TILE, TILE)


def inward_block(packed, slot_ids, counts, row_tiles, col_tiles):
    placed = unpack_tiles(packed, slot_ids, counts, row_tiles, col_tiles)
    return placed.transpose(0, 2, 1, 3).reshape(row_tiles * TILE, col_tiles * TILE)


def outward_block(packed, slot_ids, counts, row_tiles, col_tiles):
    placed = unpack_tiles(packed, slot_ids, counts, row_tiles, col_tiles)
    return placed.transpose(1, 2, 0, 3).reshape(col_tiles * TILE, row_tiles * TILE)


def gather_features(tokens, norm_gain):
    n_dp = lax.axis_size("dp")
    rows = tokens.shape[0]
    normed = normalize(tokens, norm_gain)
    mine = lax.all_to_all(
        normed.reshape(rows, n_dp, D // n_dp).transpose(1, 0, 2), "dp", 0, 0, tiled=True
    )
    mine = lax.all_gather(mine, "tensor", axis=1, tiled=True)
    return mine.reshape(n_dp * lax.axis_size("tensor") * rows, D // n_dp)


def spread_rows(part):
    part = lax.all_to_all(part.astype(jnp.bfloat16), "dp", 0, 1, tiled=True)
    return lax.psum_scatter(part, "tensor", scatter_dimension=0, tiled=True)


def swiglu(gate, upward):
    gate = gate.astype(jnp.float32)
    return (jax.nn.silu(gate) * upward.astype(jnp.float32)).astype(jnp.bfloat16)


def local_plain(tokens, norm_gain, gate_tiles, up_tiles, down_tiles, tile_ids, tile_counts):
    row_tiles = D // (TILE * lax.axis_size("dp"))
    col_tiles = FF // (TILE * lax.axis_size("tensor"))
    ids, counts = tile_ids[0, 0], tile_counts[0, 0]
    mine = gather_features(tokens, norm_gain)
    gate_block = inward_block(gate_tiles[0, 0], ids[0], counts[0], row_tiles, col_tiles)
    up_block = inward_block(up_tiles[0, 0], ids[1], counts[1], row_tiles, col_tiles)
    down_block = outward_block(down_tiles[0, 0], ids[2], counts[2], row_tiles, col_tiles)
    gate = jnp.dot(mine, gate_block, preferred_element_type=jnp.float32)
    gate = lax.psum_scatter(gate, "dp", scatter_dimension=0, tiled=True)
    upward = jnp.dot(mine, up_block, preferred_element_type=jnp.float32)
    upward = lax.psum_scatter(upward, "dp", scatter_dimension=0, tiled=True)
    hidden = lax.all_gather(swiglu(gate, upward), "dp", axis=0, tiled=True)
    return spread_rows(jnp.dot(hidden, down_block, preferred_element_type=jnp.float32))


LAG = 3
WIDE = 512


def flow_kernel(
    n_dp, n_tensor, row_tiles, col_tiles,
    tokens_in, gain, ids, counts, gate_p, up_p, down_p, out,
    normed, order, packed, gate_t, up_t, down_t, inward_w, down_w,
    xa, xg, xp, part, pair, chain, hid, acc, tail, tail_in, mixed, back, load_s,
    head_s, head_r, row_s, row_r, pair_s, pair_r, chain_s, chain_r,
    hid_s, hid_r, core_s, core_r, tail_s, tail_r, back_s, back_r,
):
    me, mt = lax.axis_index("dp"), lax.axis_index("tensor")
    z, core = me // 2, me % 2
    chips = n_dp // 2
    last = chips - 1
    groups = part.shape[0]
    rows, width = xa.shape[1], xa.shape[2]
    other = 1 - core
    buddy = z * 2 + other
    hops = ((last - z, z - 1), (z, z + 1))

    barrier = pltpu.get_barrier_semaphore()
    for d in range(1, n_dp):
        pl.semaphore_signal(
            barrier, inc=1, device_id=((me + d) % n_dp, mt), device_id_type=MESH
        )
    for d in range(1, n_tensor):
        pl.semaphore_signal(
            barrier, inc=1, device_id=(me, (mt + d) % n_tensor), device_id_type=MESH
        )
    loads = [
        pltpu.make_async_copy(source, packed.at[i], load_s.at[i])
        for i, source in enumerate((gate_p, up_p, down_p))
    ]
    for load in loads:
        load.start()

    wide = tokens_in[...].astype(jnp.float32)
    meansq = jnp.mean(wide * wide, axis=-1, keepdims=True)
    normed[...] = (wide * lax.rsqrt(meansq + 1e-05) * gain[...].reshape(1, D)).astype(jnp.bfloat16)
    source = lax.broadcasted_iota(jnp.int32, (256, 256), 0)
    place = lax.broadcasted_iota(jnp.int32, (256, 256), 1)
    inner = place & (TILE - 1)
    wanted = place - inner + 2 * (inner & (TILE // 2 - 1)) + (inner >> 5)
    order[...] = (source == wanted).astype(jnp.bfloat16)
    pl.semaphore_wait(barrier, n_dp + n_tensor - 2)

    pairs = TILE // 2
    blocks = col_tiles // 8
    tiles = row_tiles * col_tiles
    slots = packed.shape[1]
    low = lax.broadcasted_iota(jnp.int32, (pairs, 128), 1) < TILE

    def place_tiles(which, spread, at):
        tile = lax.broadcasted_iota(jnp.int32, (tiles, slots), 0)
        slot = lax.broadcasted_iota(jnp.int32, (tiles, slots), 1)
        hit = (tile == ids[which]) & (slot < counts[0, 0, which])
        columns = pl.ds(pl.multiple_of(at * WIDE, WIDE), WIDE)
        placed = jnp.dot(
            hit.astype(jnp.bfloat16), packed[which, :, columns], preferred_element_type=jnp.float32
        )
        for sub in range(WIDE // 128):
            for block in range(tiles // 8):
                start = block * pairs * 8 + (at * (WIDE // 128) + sub) * 8
                spread[pl.ds(pl.multiple_of(start, 8), 8), :] = placed[
                    block * 8 : block * 8 + 8, sub * 128 : sub * 128 + 128
                ]

    def place_all(which, spread):
        def body(at, carry):
            place_tiles(which, spread, at)
            return carry

        lax.fori_loop(0, TILE * TILE // WIDE, body, 0)

    def tile_at(spread, n, row, sub):
        start = (row * blocks + n // 4) * pairs * 8 + (n % 4) * 2 + sub
        return spread[pl.ds(start, pairs, stride=8), :]

    def join(left, right):
        even = jnp.where(low, left, pltpu.roll(right, TILE, 1))
        odd = jnp.where(low, pltpu.roll(left, TILE, 1), right)
        return even.astype(jnp.bfloat16), odd.astype(jnp.bfloat16)

    def build_inward(n):
        for which, spread in enumerate((gate_t, up_t)):
            for row in range(row_tiles):
                both = join(tile_at(spread, n, row, 0), tile_at(spread, n, row, 1))
                for odd in range(2):
                    at = row * TILE + odd * pairs
                    inward_w[at : at + pairs, which * 128 : which * 128 + 128] = both[odd]

    def build_down(n, slot):
        for sub in range(2):
            for half in range(row_tiles // 2):
                both = join(
                    tile_at(down_t, n, 2 * half, sub), tile_at(down_t, n, 2 * half + 1, sub)
                )
                for odd in range(2):
                    at = sub * TILE + odd * pairs
                    down_w[slot, at : at + pairs, half * 128 : half * 128 + 128] = both[odd]

    def send(src, dst, send_sem, recv_sem, dp, tensor):
        return pltpu.make_async_remote_copy(
            src_ref=src, dst_ref=dst, send_sem=send_sem, recv_sem=recv_sem,
            device_id=(dp, tensor), device_id_type=MESH,
        )

    def slab(index):
        return pl.ds(pl.multiple_of(index * width, width), width)

    def head(d):
        to = (me + d) % n_dp
        return send(normed.at[:, slab(to)], xa.at[me], head_s.at[d], head_r.at[d], to, mt)

    def row(d):
        return send(xa, xg.at[mt], row_s.at[d], row_r.at[d], me, (mt + d) % n_tensor)

    for d in range(1, n_dp):
        head(d).start()
    xa[me] = normed[:, slab(me)]
    loads[0].wait()
    place_all(0, gate_t)
    for d in range(1, n_dp):
        head(d).wait_recv()
    for d in range(1, n_tensor):
        row(d).start()
    xg[mt] = xa[...]
    loads[1].wait()
    place_all(1, up_t)
    loads[2].wait()
    place_all(2, down_t)
    acc[...] = jnp.zeros_like(acc)
    for d in range(1, n_tensor):
        row(d).wait_recv()
    tokens = n_tensor * n_dp * rows
    quarter = tokens // 4
    for at in range(0, width, 256):
        xp[:, at : at + 256] = jnp.dot(
            xg[:, :, :, at : at + 256].reshape(tokens, 256),
            order[...],
            preferred_element_type=jnp.float32,
        ).astype(jnp.bfloat16)

    def pair_copy(n):
        return send(part.at[n, :, other], pair.at[n], pair_s.at[n], pair_r.at[n], buddy, mt)

    def chain_copy(n, h):
        return send(
            part.at[n, h, core], chain.at[n, h], chain_s.at[n, h], chain_r.at[n, h],
            jnp.clip(hops[h][1], 0, last) * 2 + core, mt,
        )

    def hid_copy(n, h):
        to = jnp.clip(hops[1 - h][1], 0, last) * 2 + core
        return send(
            hid.at[n, h, core], hid.at[n, h, core], hid_s.at[n, h], hid_r.at[n, h], to, mt
        )

    def core_copy(n, h):
        return send(
            hid.at[n, h, core], hid.at[n, h, core], core_s.at[n, h], core_r.at[n, h], buddy, mt
        )

    def project(n):
        build_inward(n)
        value = jnp.dot(xp[...], inward_w[...], preferred_element_type=jnp.float32)
        part[n] = value.astype(jnp.bfloat16).reshape(2, 2, quarter, 256)
        pair_copy(n).start()

    def inside(n):
        return (n >= 0) & (n < groups)

    ahead = 2
    for n in range(ahead):
        project(jnp.int32(n))
    nearest = jnp.minimum(z, last - z)
    farthest = jnp.maximum(z, last - z)

    def step(s, carry):
        @pl.when(inside(s - LAG * nearest))
        def _():
            pair_copy(s - LAG * nearest).wait_recv()

        for h in range(2):
            position = hops[h][0]
            n = s - LAG * position

            @pl.when(inside(n))
            def _():
                def own():
                    return part[n, h, core].astype(jnp.float32) + pair[n, h].astype(jnp.float32)

                @pl.when(position > 0)
                def _():
                    chain_copy(n, h).wait_recv()

                @pl.when(position == 0)
                def _():
                    part[n, h, core] = own().astype(jnp.bfloat16)

                @pl.when((position > 0) & (position < last))
                def _():
                    part[n, h, core] = (own() + chain[n, h].astype(jnp.float32)).astype(jnp.bfloat16)

                @pl.when(position < last)
                def _():
                    chain_copy(n, h).start()

                @pl.when(position == last)
                def _():
                    total = own() + chain[n, h].astype(jnp.float32)
                    gate = total[:, :128]
                    value = gate / (1.0 + jnp.exp(-gate)) * total[:, 128:]
                    hid[n, h, core] = jnp.dot(
                        value.astype(jnp.bfloat16), order[:128, :128], preferred_element_type=jnp.float32
                    ).astype(jnp.bfloat16)

        for h in range(2):
            distance = last - hops[h][0]
            n = s - LAG * (last + distance)

            @pl.when(inside(n))
            def _():
                @pl.when(distance > 0)
                def _():
                    hid_copy(n, h).wait_recv()

                @pl.when(distance < last)
                def _():
                    hid_copy(n, h).start()

                core_copy(n, h).start()

        @pl.when(s + ahead < groups)
        def _():
            project(s + ahead)

        done = s - LAG * (last + farthest) - 1

        @pl.when(inside(done))
        def _():
            for h in range(2):
                core_copy(done, h).wait_recv()
            build_down(done, done % 2)

            @pl.when(done % 2 == 1)
            def _():
                both = jnp.concatenate(
                    [hid[done - 1].reshape(tokens, 128), hid[done].reshape(tokens, 128)], axis=1
                )
                acc[...] += jnp.dot(
                    both, down_w[...].reshape(256, width), preferred_element_type=jnp.float32
                )

        return carry

    lax.fori_loop(0, groups + 2 * LAG * last + 1, step, 0)

    tail[...] = acc[...].astype(jnp.bfloat16).reshape(tail.shape)

    def tail_copy(d):
        to = (mt + d) % n_tensor
        return send(tail.at[to], tail_in.at[mt], tail_s.at[d], tail_r.at[d], me, to)

    def back_copy(d):
        to = (me + d) % n_dp
        return send(mixed.at[to], back.at[me], back_s.at[d], back_r.at[d], to, mt)

    for d in range(1, n_tensor):
        tail_copy(d).start()
    tail_in[mt] = tail[mt]

    def drain(n, carry):
        pair_copy(n).wait_send()
        for h in range(2):
            core_copy(n, h).wait_send()

            @pl.when(hops[h][0] < last)
            def _():
                chain_copy(n, h).wait_send()

            @pl.when(last - hops[h][0] < last)
            def _():
                hid_copy(n, h).wait_send()

        return carry

    lax.fori_loop(0, groups, drain, 0)
    for d in range(1, n_dp):
        head(d).wait_send()
    for d in range(1, n_tensor):
        row(d).wait_send()
    for d in range(1, n_tensor):
        tail_copy(d).wait_recv()
    total = tail_in[0].astype(jnp.float32)
    for t in range(1, n_tensor):
        total += tail_in[t].astype(jnp.float32)
    mixed[...] = total.astype(jnp.bfloat16).reshape(mixed.shape)
    for d in range(1, n_dp):
        back_copy(d).start()
    back[me] = mixed[me]

    for d in range(1, n_dp):
        back_copy(d).wait_recv()
        back_copy(d).wait_send()
    for d in range(1, n_tensor):
        tail_copy(d).wait_send()
    for p in range(n_dp):
        out[:, p * width : p * width + width] = back[p]


def flow(tokens, gain, ids, counts, gate_p, up_p, down_p, n_dp, n_tensor, row_tiles, col_tiles):
    groups = col_tiles // 2
    width = row_tiles * TILE
    rows = tokens.shape[0]
    total = rows * n_dp * n_tensor
    quarter = total // 4
    tiles = row_tiles * col_tiles
    half = jnp.bfloat16
    dma = pltpu.SemaphoreType.DMA
    vmem = pl.BlockSpec(memory_space=pltpu.VMEM)
    return pl.pallas_call(
        lambda *refs: flow_kernel(n_dp, n_tensor, row_tiles, col_tiles, *refs),
        out_shape=jax.ShapeDtypeStruct(tokens.shape, half),
        in_specs=[vmem] * 3 + [pl.BlockSpec(memory_space=pltpu.SMEM)] + [pl.BlockSpec(memory_space=pl.ANY)] * 3,
        out_specs=vmem,
        scratch_shapes=[
            pltpu.VMEM(tokens.shape, half),
            pltpu.VMEM((256, 256), half),
            pltpu.VMEM((3,) + gate_p.shape, half),
            pltpu.VMEM((tiles * TILE // 2, 128), jnp.float32),
            pltpu.VMEM((tiles * TILE // 2, 128), jnp.float32),
            pltpu.VMEM((tiles * TILE // 2, 128), jnp.float32),
            pltpu.VMEM((width, 256), half),
            pltpu.VMEM((2, 128, width), half),
            pltpu.VMEM((n_dp, rows, width), half),
            pltpu.VMEM((n_tensor, n_dp, rows, width), half),
            pltpu.VMEM((total, width), half),
            pltpu.VMEM((groups, 2, 2, quarter, 256), half),
            pltpu.VMEM((groups, 2, quarter, 256), half),
            pltpu.VMEM((groups, 2, quarter, 256), half),
            pltpu.VMEM((groups, 2, 2, quarter, 128), half),
            pltpu.VMEM((total, width), jnp.float32),
            pltpu.VMEM((n_tensor, n_dp * rows, width), half),
            pltpu.VMEM((n_tensor, n_dp * rows, width), half),
            pltpu.VMEM((n_dp, rows, width), half),
            pltpu.VMEM((n_dp, rows, width), half),
            dma((3,)),
            dma((n_dp,)), dma((n_dp,)), dma((n_tensor,)), dma((n_tensor,)),
            dma((groups,)), dma((groups,)), dma((groups, 2)), dma((groups, 2)),
            dma((groups, 2)), dma((groups, 2)), dma((groups, 2)), dma((groups, 2)),
            dma((n_tensor,)), dma((n_tensor,)), dma((n_dp,)), dma((n_dp,)),
        ],
        compiler_params=pltpu.CompilerParams(
            collective_id=0, has_side_effects=True, vmem_limit_bytes=60 << 20
        ),
        cost_estimate=pl.CostEstimate(
            flops=9 * 10**9, bytes_accessed=6 << 20, transcendentals=10**6
        ),
        name="flow",
    )(tokens, gain, ids, counts, gate_p, up_p, down_p)


def local(tokens, norm_gain, gate_tiles, up_tiles, down_tiles, tile_ids, tile_counts):
    n_dp, n_tensor = lax.axis_size("dp"), lax.axis_size("tensor")
    row_tiles = D // (TILE * n_dp)
    col_tiles = FF // (TILE * n_tensor)
    if col_tiles % 8 != 0 or row_tiles % 4 != 0 or n_tensor != 4 or n_dp != 8:
        return local_plain(
            tokens, norm_gain, gate_tiles, up_tiles, down_tiles, tile_ids, tile_counts
        )
    return flow(
        tokens, norm_gain, tile_ids[0, 0][:, None, :], tile_counts,
        gate_tiles[0, 0], up_tiles[0, 0], down_tiles[0, 0],
        n_dp, n_tensor, row_tiles, col_tiles,
    )


def solution(mesh):
    return jax.shard_map(
        local,
        mesh=mesh,
        in_specs=(
            P(("dp", "tensor"), None),
            P(),
            P("tensor", "dp", None, None),
            P("tensor", "dp", None, None),
            P("tensor", "dp", None, None),
            P("tensor", "dp", None, None),
            P("tensor", "dp", None),
        ),
        out_specs=P(("dp", "tensor"), None),
        check_vma=False,
    )
```
